512 devices in a mesh: dp: 16 (over y, core), mp: 32 (over x, z).
Axes of the slice: x: 4, y: 8, z: 8, core: 2. Of those that a mesh axis runs over, the one named last changes fastest.
Arguments:
- layer_input: bfloat16 [8192, 4096], P('dp', 'mp'), may hold values from -6 to 6
- gate_pre: bfloat16 [8192, 14336], P('dp', 'mp'), may hold values from -6 to 6
- up_pre: bfloat16 [8192, 14336], P('dp', 'mp'), may hold values from -6 to 6
- out_grad: bfloat16 [8192, 4096], P('dp', 'mp'), may hold values from -36 to 36
- w_down: bfloat16 [14336, 4096], P('mp'), may hold values from -0.09375 to 0.09375
- proj_input: bfloat16 [4096, 64], P('mp'), may hold values from -4 to 4
- proj_hidden: bfloat16 [14336, 64], P('mp'), may hold values from -4 to 4
- proj_gate: bfloat16 [14336, 64], P('mp'), may hold values from -0.046875 to 0.046875
- proj_upward: bfloat16 [14336, 64], P('mp'), may hold values from -0.046875 to 0.046875
- proj_output: bfloat16 [64, 4096], P(None, 'mp'), may hold values from -0.09375 to 0.09375
- seq_ids: int32 [16, 512], P('dp'), may hold values from 0 to 7, never falling along the last dimension, each value on 1 to 128 neighbouring positions
Outputs:
- features: float32 [128, 3, 4096], P('dp', None, 'mp')
The draws below stay inside these ranges and needn't reach their ends.
Inputs may be any that keep to these rules, and one draw needn't show every extreme that they name: `seq_ids`: within each row the ids never fall and every id appears; every sequence has 1 to 128 tokens and some sequence of each row has exactly 128.
All inputs are finite; a program needn't handle non-finite values.
Results may differ from the reference program's by a relative error of at most 0.0029.
Values may be sent and summed in bfloat16 or wider, within the bound.
No kernel may reach another device: no remote copies, remote signals or barrier semaphores. Data moves between devices by JAX's collectives and lax.ppermute only.
A program may use at most 64 MiB of HBM per device.

```python
import math
import jax
import jax.numpy as jnp
import numpy as np
from jax import lax

D = 4096
FF = 14336
RANK = 64
SEQ_LEN = 64
TOK_DEV = 512
SEQ_DEV = 8
LMAX = 128
GROUPS = 16
TOKENS = 8192
SEQS = 128


def column_projection(key, fan_rows, low_scale, high_scale):
    first_key, second_key = jax.random.split(key)
    base = jnp.clip(jax.random.normal(first_key, (fan_rows, RANK), jnp.float32), -4.0, 4.0)
    rising = jnp.sqrt(1.0 + 2.0 * jnp.arange(RANK, dtype=jnp.float32) / (RANK - 1))
    spread = jnp.exp(jax.random.uniform(second_key, (RANK,), jnp.float32, math.log(low_scale), math.log(high_scale)))
    return (base * (rising * spread)[None, :] / math.sqrt(fan_rows)).astype(jnp.bfloat16)


def draw_proj_input(key, part):
    key = jax.random.fold_in(key, 21)
    return column_projection(key, D, 0.3, 3.0)


def draw_proj_hidden(key, part):
    key = jax.random.fold_in(key, 31)
    return column_projection(key, FF, 0.3, 3.0)


def draw_out_grad(key, part):
    key = jax.random.fold_in(key, 11)
    first_key, second_key = jax.random.split(key, 2)
    blocks = TOKENS // SEQ_LEN
    spread = jnp.exp(jax.random.uniform(second_key, (blocks,), jnp.float32, 0.0, math.log(10.0)))
    base = jnp.clip(jax.random.normal(first_key, (TOKENS, D), jnp.float32), -4.0, 4.0)
    positions = jnp.arange(TOKENS, dtype=jnp.int32)
    rising = 1.0 + 2.0 * positions.astype(jnp.float32) / (TOKENS - 1)
    row_scale = 0.3 * rising * spread[positions // SEQ_LEN]
    return (base * row_scale[:, None]).astype(jnp.bfloat16)


def steps_of(stream_key, extent, cuts, smallest, high):
    gain, own = 1.0, jax.random.fold_in(stream_key, 6)
    for position, blocks in cuts:
        steps = jnp.exp(jax.random.uniform(jax.random.fold_in(own, position), (blocks,), jnp.float32, smallest / len(cuts), high / len(cuts)))
        gain = gain * jnp.repeat(steps, extent[position] // blocks).reshape([-1 if axis == position else 1 for axis in range(len(extent))])
    return gain


def split_up(amount, total, bound, skew):
    loads = [(1 << 20) // math.isqrt(standing ** skew) + 1 for standing in range(2, amount + 1)]
    spare, holding = total - bound - (amount - 1), [1] * (amount - 1)
    while spare > 0:
        candidates = [i for i in range(amount - 1) if holding[i] < bound]
        whole, remaining = sum([loads[i] for i in candidates]), spare
        for i in candidates:
            more = min(bound - holding[i], max(1, remaining * loads[i] // whole), spare)
            holding[i] = holding[i] + more
            spare = spare - more
    return np.array([bound] + holding)


def ragged(rng, count, total, bound, lean):
    if count == 2:
        one = jax.random.randint(rng, (), max(1, total - bound), min(bound, total - 1) + 1)
        return jnp.stack([one, total - one])
    lengths = jnp.asarray(split_up(count, total, bound, lean), jnp.int32)
    couples = (count - 1) // 2
    donor, sink = lengths[1:1 + 2 * couples:2], lengths[2:2 + 2 * couples:2]
    slack = jnp.minimum(donor - 1, bound - sink)
    passed = jax.random.randint(jax.random.fold_in(rng, 1), (couples,), 0, 1 << 20) % (slack + 1)
    lengths = lengths.at[1:1 + 2 * couples:2].set(donor - passed).at[2:2 + 2 * couples:2].set(sink + passed)
    return lengths[jax.random.permutation(jax.random.fold_in(rng, 2), count)]


def bell_draw(own_key, extent, scale, bound, pieces=(), kind=jnp.bfloat16):
    entries = scale * jax.random.normal(own_key, extent, jnp.float32)
    if pieces:
        entries = entries * steps_of(own_key, extent, pieces, -0.22, 0.18)
    return jnp.clip(entries, -bound, bound).astype(kind)


def setup_inputs(seed: int = 0) -> dict:
    keys = jax.random.split(jax.random.key(seed), 12)
    layer_input = bell_draw(keys[0], (TOKENS, D), 1.0, 6.0, ((0, 16), (1, 32)))
    gate_pre = bell_draw(keys[1], (TOKENS, FF), 1.0, 6.0, ((0, 16), (1, 32)))
    up_pre = bell_draw(keys[2], (TOKENS, FF), 1.0, 6.0, ((0, 16), (1, 32)))
    out_grad = draw_out_grad(jax.random.fold_in(keys[11], 71), 0)
    w_down = bell_draw(keys[4], (FF, D), D ** -0.5, 0.09375, ((0, 32),))
    proj_input = draw_proj_input(jax.random.fold_in(keys[11], 71), 0)
    proj_hidden = draw_proj_hidden(jax.random.fold_in(keys[11], 71), 0)
    proj_gate = bell_draw(keys[7], (FF, RANK), FF ** -0.5, 0.046875, ((0, 32),))
    proj_upward = bell_draw(keys[8], (FF, RANK), FF ** -0.5, 0.046875, ((0, 32),))
    proj_output = bell_draw(keys[9], (RANK, D), D ** -0.5, 0.09375, ((1, 32),))
    seq_ids = jax.vmap(lambda own: jnp.searchsorted(jnp.cumsum(ragged(own, SEQ_DEV, TOK_DEV, LMAX, 1)), jnp.arange(TOK_DEV), side="right"))(jax.random.split(keys[10], GROUPS)).reshape((GROUPS, TOK_DEV)).astype(jnp.int32)
    return {"layer_input": layer_input, "gate_pre": gate_pre, "up_pre": up_pre, "out_grad": out_grad, "w_down": w_down, "proj_input": proj_input, "proj_hidden": proj_hidden, "proj_gate": proj_gate, "proj_upward": proj_upward, "proj_output": proj_output, "seq_ids": seq_ids}


def silu_parts(gate_value):
    sigmoid_v = jax.nn.sigmoid(gate_value)
    return (gate_value * sigmoid_v, sigmoid_v * (1.0 + gate_value * (1.0 - sigmoid_v)))

def outer_sum(member, left_side, right_side):
    weighted = member[:, :, None] * left_side[None, :, :]
    joined = jnp.einsum('sti,tj->sij', weighted, right_side, precision=lax.Precision.HIGHEST)
    return joined.reshape(member.shape[0], -1)

def reference(layer_input, gate_pre, up_pre, out_grad, w_down, proj_input, proj_hidden, proj_gate, proj_upward, proj_output, seq_ids):
    contract = (((1,), (1,)), ((), ()))

    def one_group(blocks):
        group_input, group_gate, group_up, group_grad, seq_row = blocks
        gate_value = group_gate.astype(jnp.float32)
        up_value = group_up.astype(jnp.float32)
        activated, slope_value = silu_parts(gate_value)
        hidden = (activated * up_value).astype(jnp.bfloat16)
        hidden_grad = lax.dot_general(group_grad, w_down, contract, preferred_element_type=jnp.float32)
        gate_grad = (hidden_grad * up_value * slope_value).astype(jnp.bfloat16)
        upward_grad = (hidden_grad * activated).astype(jnp.bfloat16)
        in_factor = jnp.dot(group_input, proj_input, preferred_element_type=jnp.float32)
        hid_factor = jnp.dot(hidden, proj_hidden, preferred_element_type=jnp.float32)
        gate_factor = jnp.dot(gate_grad, proj_gate, preferred_element_type=jnp.float32)
        up_factor = jnp.dot(upward_grad, proj_upward, preferred_element_type=jnp.float32)
        out_factor = lax.dot_general(group_grad, proj_output, contract, preferred_element_type=jnp.float32)
        member = (seq_row[None, :] == jnp.arange(SEQ_DEV, dtype=jnp.int32)[:, None]).astype(jnp.float32)
        return jnp.stack([outer_sum(member, in_factor, gate_factor), outer_sum(member, in_factor, up_factor), outer_sum(member, hid_factor, out_factor)], axis=1)
    raw_feat = lax.map(one_group, (layer_input.reshape(GROUPS, TOK_DEV, D), gate_pre.reshape(GROUPS, TOK_DEV, FF), up_pre.reshape(GROUPS, TOK_DEV, FF), out_grad.reshape(GROUPS, TOK_DEV, D), seq_ids))
    raw_feat = raw_feat.reshape(SEQS, 3, RANK * RANK)
    scale_value = lax.rsqrt(lax.optimization_barrier(jnp.mean(raw_feat * raw_feat, axis=(0, 2))) + 1e-06)
    return raw_feat * scale_value[None, :, None]
```

```python
import jax
import jax.numpy as jnp
from jax import lax
from jax.sharding import PartitionSpec as P

SEQ_DEV = 8
NX = 4
NZ = 8
X_GROUPS = [[x * NZ + z for x in range(NX)] for z in range(NZ)]
Z_GROUPS = [[x * NZ + z for z in range(NZ)] for x in range(NX)]
CONTRACT = (((1,), (1,)), ((), ()))


def split_hi_lo(value):
    high = lax.reduce_precision(value, 8, 7)
    return high.astype(jnp.bfloat16), (value - high).astype(jnp.bfloat16)


def x_shift(step):
    return [
        (x * NZ + z, ((x + step) % NX) * NZ + z) for x in range(NX) for z in range(NZ)
    ]


def hidden_part(gate_pre, up_pre):
    gate_value = gate_pre.astype(jnp.float32)
    up_value = up_pre.astype(jnp.float32)
    sigmoid_v = jax.nn.sigmoid(gate_value)
    activated = gate_value * sigmoid_v
    slope = sigmoid_v * (1.0 + gate_value * (1.0 - sigmoid_v))
    return activated, slope, up_value


def per_device(
    layer_input,
    gate_pre,
    up_pre,
    out_grad,
    w_down,
    proj_input,
    proj_hidden,
    proj_gate,
    proj_upward,
    proj_output,
    seq_ids,
):
    tokens, width = out_grad.shape
    half = tokens // 2
    rank = proj_input.shape[1]
    mp_size = lax.axis_size("mp")
    dp_size = lax.axis_size("dp")
    own_tokens = tokens // mp_size
    position = lax.axis_index("mp")
    x_pos = position // NZ

    in_part = jnp.dot(layer_input, proj_input, preferred_element_type=jnp.float32)
    out_part = lax.dot_general(out_grad, proj_output, CONTRACT, preferred_element_type=jnp.float32)
    both = jnp.concatenate([in_part, out_part], axis=1)

    high, low = split_hi_lo(both)
    share = tokens // NX
    sent = jnp.concatenate(
        [
            jnp.broadcast_to(out_grad[None, half:], (NX, half, width)),
            high.reshape(NX, share, 2 * rank),
            low.reshape(NX, share, 2 * rank),
        ],
        axis=1,
    )
    got = lax.all_to_all(sent, "mp", 0, 0, axis_index_groups=X_GROUPS)
    late_x = got[:, :half]
    both = jnp.sum(
        got[:, half : half + share].astype(jnp.float32) + got[:, half + share :].astype(jnp.float32), axis=0
    )
    late = lax.all_gather(late_x, "mp", axis=0, axis_index_groups=Z_GROUPS)

    high, low = split_hi_lo(both)
    sent = jnp.concatenate(
        [
            jnp.broadcast_to(out_grad[None, :half], (NZ, half, width)),
            high.reshape(NZ, own_tokens, 2 * rank),
            low.reshape(NZ, own_tokens, 2 * rank),
        ],
        axis=1,
    )
    got = lax.all_to_all(sent, "mp", 0, 0, axis_index_groups=Z_GROUPS)
    early_z = got[:, :half]
    both = jnp.sum(
        got[:, half : half + own_tokens].astype(jnp.float32) + got[:, half + own_tokens :].astype(jnp.float32),
        axis=0,
    )
    early = [early_z] + [lax.ppermute(early_z, "mp", x_shift(step)) for step in range(1, NX)]

    both = lax.all_to_all(jnp.broadcast_to(both[None], (mp_size, own_tokens, 2 * rank)), "mp", 0, 0)
    both = both.reshape(tokens, 2 * rank)
    in_factor, out_factor = both[:, :rank], both[:, rank:]

    member = (seq_ids[0][None, :] == jnp.arange(SEQ_DEV, dtype=jnp.int32)[:, None]).astype(jnp.float32)
    activated, slope, up_value = hidden_part(gate_pre, up_pre)
    hidden = (activated * up_value).astype(jnp.bfloat16)
    hid_part = jnp.dot(hidden, proj_hidden, preferred_element_type=jnp.float32)
    left_in = (in_factor.T[:, None, :] * member[None]).reshape(rank * SEQ_DEV, tokens)
    left_hid = hid_part.T.reshape(rank // 2, 2, 1, tokens) * member[None, None]
    down_raw = [
        jnp.dot(
            left_hid[:, i].reshape(rank // 2 * SEQ_DEV, tokens), out_factor, precision=lax.Precision.HIGHEST
        ).reshape(mp_size, SEQ_DEV, rank)
        for i in range(2)
    ]
    down_raw = jnp.concatenate(down_raw, axis=2)

    w_blocks = w_down.reshape(w_down.shape[0], NX, NZ, width)
    early_grad = 0.0
    for step in range(NX):
        w_step = lax.dynamic_index_in_dim(w_blocks, (x_pos - step) % NX, 1, keepdims=False)
        rows = early[step].transpose(1, 0, 2).reshape(half, NZ * width)
        early_grad += lax.dot_general(
            rows, w_step.reshape(-1, NZ * width), CONTRACT, preferred_element_type=jnp.float32
        )
    late_rows = late.transpose(2, 1, 0, 3).reshape(half, NX * NZ * width)
    late_grad = lax.dot_general(late_rows, w_down, CONTRACT, preferred_element_type=jnp.float32)
    hidden_grad = jnp.concatenate([early_grad, late_grad], axis=0)
    gate_grad = (hidden_grad * up_value * slope).astype(jnp.bfloat16)
    upward_grad = (hidden_grad * activated).astype(jnp.bfloat16)
    gate_part = jnp.dot(gate_grad, proj_gate, preferred_element_type=jnp.float32)
    up_part = jnp.dot(upward_grad, proj_upward, preferred_element_type=jnp.float32)
    paired = jnp.dot(
        left_in, jnp.concatenate([gate_part, up_part], axis=1), precision=lax.Precision.HIGHEST
    )
    sent = jnp.concatenate([paired.reshape(mp_size, 2 * SEQ_DEV, 2 * rank), down_raw], axis=1)
    got = jnp.sum(lax.all_to_all(sent, "mp", 0, 0), axis=0)
    paired, down = got[: 2 * SEQ_DEV], got[2 * SEQ_DEV :]
    paired = paired.reshape(2, SEQ_DEV, 2, rank).transpose(1, 2, 0, 3).reshape(SEQ_DEV, 2, 2 * rank)
    raw = jnp.concatenate([paired, down[:, None]], axis=1)

    squares = jnp.sum(raw * raw, axis=(0, 2))
    squares = jnp.pad(squares, (0, 125)).reshape(1, 1, 128)
    for axis, size in (("mp", mp_size), ("dp", dp_size)):
        squares = jnp.sum(
            lax.all_to_all(jnp.broadcast_to(squares, (size, 1, 128)), axis, 0, 0), axis=0, keepdims=True
        )
    entries = SEQ_DEV * dp_size * rank * rank
    scale = lax.rsqrt(squares[0, 0, :3] / entries + 1e-06)
    return raw * scale[None, :, None]


def solution(mesh):
    in_specs = (
        P("dp", "mp"),
        P("dp", "mp"),
        P("dp", "mp"),
        P("dp", "mp"),
        P("mp", None),
        P("mp", None),
        P("mp", None),
        P("mp", None),
        P("mp", None),
        P(None, "mp"),
        P("dp", None),
    )
    out_specs = P("dp", None, "mp")
    return jax.shard_map(
        per_device, mesh=mesh, in_specs=in_specs, out_specs=out_specs, check_vma=False
    )
```

```python
import jax
import jax.numpy as jnp
from jax import lax
from jax.experimental import pallas as pl
from jax.experimental.pallas import tpu as pltpu
from jax.sharding import PartitionSpec as P

SEQ_DEV = 8
NX = 4
NZ = 8
X_GROUPS = [[x * NZ + z for x in range(NX)] for z in range(NZ)]
CONTRACT = (((1,), (1,)), ((), ()))


def z_shift(step):
    return [
        (x * NZ + z, x * NZ + (z + step) % NZ) for x in range(NX) for z in range(NZ)
    ]


def grad_kernel(pieces, carried, place_ref, *refs):
    piece_refs, refs = refs[:pieces], refs[pieces:]
    widths = [piece.shape[0] for piece in piece_refs]
    w_refs, refs = refs[: sum(widths)], refs[sum(widths) :]
    rows = jnp.concatenate([piece[i] for piece, n in zip(piece_refs, widths) for i in range(n)], axis=1)
    weights = jnp.concatenate([w[...] for w in w_refs], axis=1)
    total = lax.dot_general(rows, weights, CONTRACT, preferred_element_type=jnp.float32)
    if carried:
        total = refs[0][...] + total
    refs[-1][...] = total


def add_grad(places, pieces, w_down, carried=None):
    hidden, _ = w_down.shape
    tokens, width = pieces[0][0].shape[1:]

    def whole(shape):
        return pl.BlockSpec(shape, lambda i, place, n=len(shape): (0,) * n)

    specs, w_specs = [], []
    for k, (block, first) in enumerate(pieces):
        specs.append(whole(block.shape))
        for x in range(first, first + block.shape[0]):
            w_specs.append(
                pl.BlockSpec((hidden, width), lambda i, place, k=k, x=x: (0, x * NZ + place[k]))
            )
    operands = [block for block, _ in pieces] + [w_down] * len(w_specs)
    specs += w_specs
    aliases = {}
    if carried is not None:
        aliases = {1 + len(operands): 0}
        operands.append(carried)
        specs.append(whole((tokens, hidden)))
    return pl.pallas_call(
        lambda *refs: grad_kernel(len(pieces), carried is not None, *refs),
        out_shape=jax.ShapeDtypeStruct((tokens, hidden), jnp.float32),
        grid_spec=pltpu.PrefetchScalarGridSpec(
            num_scalar_prefetch=1,
            grid=(1,),
            in_specs=specs,
            out_specs=whole((tokens, hidden)),
        ),
        input_output_aliases=aliases,
        compiler_params=pltpu.CompilerParams(vmem_limit_bytes=32 * 1024 * 1024),
    )(places, *operands)


def hidden_part(gate_pre, up_pre):
    gate_value = gate_pre.astype(jnp.float32)
    up_value = up_pre.astype(jnp.float32)
    sigmoid_v = jax.nn.sigmoid(gate_value)
    activated = gate_value * sigmoid_v
    slope = sigmoid_v * (1.0 + gate_value * (1.0 - sigmoid_v))
    return activated, slope, up_value


def per_device(
    layer_input,
    gate_pre,
    up_pre,
    out_grad,
    w_down,
    proj_input,
    proj_hidden,
    proj_gate,
    proj_upward,
    proj_output,
    seq_ids,
):
    tokens, width = out_grad.shape
    rank = proj_input.shape[1]
    mp_size = lax.axis_size("mp")
    dp_size = lax.axis_size("dp")
    own_tokens = tokens // mp_size
    position = lax.axis_index("mp")
    z_pos = position % NZ

    in_part = jnp.dot(layer_input, proj_input, preferred_element_type=jnp.float32)
    out_part = lax.dot_general(out_grad, proj_output, CONTRACT, preferred_element_type=jnp.float32)
    both = jnp.concatenate([in_part, out_part], axis=1)

    across_x = lax.all_to_all(
        jnp.broadcast_to(out_grad[None], (NX, tokens, width)), "mp", 0, 0, axis_index_groups=X_GROUPS
    )
    blocks = {0: across_x}
    for step in range(1, NZ // 2):
        blocks[step] = lax.ppermute(blocks[step - 1], "mp", z_shift(1))
        blocks[-step] = lax.ppermute(blocks[1 - step], "mp", z_shift(-1))
    far = NZ // 2
    far_pieces = [
        (lax.ppermute(blocks[far - 1][: NX // 2], "mp", z_shift(1)), 0),
        (lax.ppermute(blocks[1 - far][NX // 2 :], "mp", z_shift(-1)), NX // 2),
    ]

    both = lax.all_to_all(both.reshape(mp_size, own_tokens, 2 * rank), "mp", 0, 0).sum(axis=0)
    both = lax.all_to_all(jnp.broadcast_to(both[None], (mp_size, own_tokens, 2 * rank)), "mp", 0, 0)
    both = both.reshape(tokens, 2 * rank)
    in_factor, out_factor = both[:, :rank], both[:, rank:]

    member = (seq_ids[0][None, :] == jnp.arange(SEQ_DEV, dtype=jnp.int32)[:, None]).astype(jnp.float32)
    activated, slope, up_value = hidden_part(gate_pre, up_pre)
    hidden = (activated * up_value).astype(jnp.bfloat16)
    hid_part = jnp.dot(hidden, proj_hidden, preferred_element_type=jnp.float32)
    left_in = (in_factor.T[:, None, :] * member[None]).reshape(rank * SEQ_DEV, tokens)
    left_hid = hid_part.T.reshape(rank // 2, 2, 1, tokens) * member[None, None]
    down_raw = [
        jnp.dot(
            left_hid[:, i].reshape(rank // 2 * SEQ_DEV, tokens), out_factor, precision=lax.Precision.HIGHEST
        ).reshape(mp_size, SEQ_DEV, rank)
        for i in range(2)
    ]
    down_raw = jnp.concatenate(down_raw, axis=2)

    def places(*steps):
        return jnp.stack([(z_pos - step) % NZ for step in steps]).astype(jnp.int32)

    hidden_grad = add_grad(places(0), [(blocks[0], 0)], w_down)
    for step in range(1, far):
        hidden_grad = add_grad(
            places(step, -step), [(blocks[step], 0), (blocks[-step], 0)], w_down, hidden_grad
        )
    hidden_grad = add_grad(places(far, far), far_pieces, w_down, hidden_grad)
    gate_grad = (hidden_grad * up_value * slope).astype(jnp.bfloat16)
    upward_grad = (hidden_grad * activated).astype(jnp.bfloat16)
    gate_part = jnp.dot(gate_grad, proj_gate, preferred_element_type=jnp.float32)
    up_part = jnp.dot(upward_grad, proj_upward, preferred_element_type=jnp.float32)
    paired = jnp.dot(
        left_in, jnp.concatenate([gate_part, up_part], axis=1), precision=lax.Precision.HIGHEST
    )
    sent = jnp.concatenate([paired.reshape(mp_size, 2 * SEQ_DEV, 2 * rank), down_raw], axis=1)
    got = jnp.sum(lax.all_to_all(sent, "mp", 0, 0), axis=0)
    paired, down = got[: 2 * SEQ_DEV], got[2 * SEQ_DEV :]
    paired = paired.reshape(2, SEQ_DEV, 2, rank).transpose(1, 2, 0, 3).reshape(SEQ_DEV, 2, 2 * rank)
    raw = jnp.concatenate([paired, down[:, None]], axis=1)

    squares = jnp.sum(raw * raw, axis=(0, 2))
    squares = jnp.pad(squares, (0, 125)).reshape(1, 1, 128)
    for axis, size in (("mp", mp_size), ("dp", dp_size)):
        squares = jnp.sum(
            lax.all_to_all(jnp.broadcast_to(squares, (size, 1, 128)), axis, 0, 0), axis=0, keepdims=True
        )
    entries = SEQ_DEV * dp_size * rank * rank
    scale = lax.rsqrt(squares[0, 0, :3] / entries + 1e-06)
    return raw * scale[None, :, None]


def solution(mesh):
    in_specs = (
        P("dp", "mp"),
        P("dp", "mp"),
        P("dp", "mp"),
        P("dp", "mp"),
        P("mp", None),
        P("mp", None),
        P("mp", None),
        P("mp", None),
        P("mp", None),
        P(None, "mp"),
        P("dp", None),
    )
    out_specs = P("dp", None, "mp")
    return jax.shard_map(
        per_device, mesh=mesh, in_specs=in_specs, out_specs=out_specs, check_vma=False
    )
```

```python
import jax
import jax.numpy as jnp
from jax import lax
from jax.experimental import pallas as pl
from jax.experimental.pallas import tpu as pltpu
from jax.sharding import PartitionSpec as P

SEQ_DEV = 8
NX = 4
NZ = 8
RING = [(0,), (1, -1), (2, -2), (3, -3), (4,)]
X_GROUPS = [[x * NZ + z for x in range(NX)] for z in range(NZ)]
Z_GROUPS = [[x * NZ + z for z in range(NZ)] for x in range(NX)]
F32, BF16 = jnp.float32, jnp.bfloat16
VMEM = pl.BlockSpec(memory_space=pltpu.VMEM)
HBM = pl.BlockSpec(memory_space=pltpu.HBM)
MIB = 1024 * 1024


def z_shift(step):
    return [(x * NZ + z, x * NZ + (z + step) % NZ) for x in range(NX) for z in range(NZ)]


def mm(left, right):
    return jnp.dot(left, right, preferred_element_type=F32)


def mm_nt(left, right):
    return lax.dot_general(left, right, (((1,), (1,)), ((), ())), preferred_element_type=F32)


def halves(value):
    high = value.astype(BF16)
    return high, (value - high.astype(F32)).astype(BF16)


def tie(value, *others):
    return lax.optimization_barrier((value, *others))[0]


def call(kernel, out_shape, specs, operands, flops, aliases=None, scratch=(), vmem=8):
    size = sum(x.size * x.dtype.itemsize for x in operands)
    return pl.pallas_call(
        kernel,
        out_shape=out_shape,
        in_specs=specs,
        out_specs=jax.tree.map(lambda _: VMEM, out_shape),
        scratch_shapes=scratch,
        input_output_aliases=aliases or {},
        cost_estimate=pl.CostEstimate(flops=flops, bytes_accessed=size, transcendentals=0),
        compiler_params=pltpu.CompilerParams(vmem_limit_bytes=vmem * MIB),
    )(*operands)


def fetch(pairs, sems):
    copies = [pltpu.make_async_copy(source, target, sems.at[k]) for k, (source, target) in enumerate(pairs)]
    for copy in copies:
        copy.start()
    return copies


def wait(copies):
    for copy in copies:
        copy.wait()


def start_kernel(
    input_hbm, grad_hbm, proj_in_hbm, proj_out_hbm, sent_ref, input_ref, grad_ref, proj_in_ref, proj_out_ref, sems
):
    wait(
        fetch(
            [
                (grad_hbm, grad_ref),
                (proj_out_hbm, proj_out_ref),
                (input_hbm, input_ref),
                (proj_in_hbm, proj_in_ref),
            ],
            sems,
        )
    )
    grad = grad_ref[...]
    both = jnp.concatenate(
        [mm_nt(proj_in_ref[...], input_ref[...]), mm_nt(proj_out_ref[...], grad)], axis=0
    )
    share = both.shape[1] // NX
    for x in range(NX):
        sent_ref[x] = jnp.concatenate([grad, *halves(both[:, x * share : (x + 1) * share])], axis=0)


def split_kernel(got_ref, block_ref, both_ref, parts_ref):
    deep = both_ref.shape[0]
    tokens = got_ref.shape[1] - 2 * deep
    both = got_ref[:, tokens : tokens + deep].astype(F32) + got_ref[:, tokens + deep :].astype(F32)
    both = jnp.sum(both, axis=0)
    both_ref[...] = both
    parts = jnp.concatenate(halves(both), axis=0)
    parts_ref[...] = parts
    block_ref[:, :tokens] = got_ref[:, :tokens]
    block_ref[:, tokens:] = parts.reshape(NX, -1, parts.shape[1])


def spread_kernel(both_ref, parts_ref, sent_ref):
    deep = both_ref.shape[0]
    both = both_ref[...] + parts_ref[:deep].astype(F32) + parts_ref[deep:].astype(F32)
    for x in range(NX):
        sent_ref[x] = both


def hidden_kernel(gate_ref, up_ref, proj_ref, activated_ref, slope_ref, hid_ref):
    gate = gate_ref[...].T.astype(F32)
    up = up_ref[...].T.astype(F32)
    sigmoid = jax.nn.sigmoid(gate)
    activated = gate * sigmoid
    activated_ref[...] = activated
    slope_ref[...] = up * (sigmoid * (1.0 + gate * (1.0 - sigmoid)))
    hid_ref[...] = mm_nt(proj_ref[...], (activated * up).astype(BF16))


def factor_kernel(both_ref, hid_ref, ids_ref, high_ref, low_ref, down_ref):
    rank, tokens = hid_ref.shape
    both = jnp.concatenate([both_ref[x] for x in range(NX)], axis=1)
    member = ids_ref[...] == lax.broadcasted_iota(jnp.int32, (SEQ_DEV, tokens), 0)

    def masked(value):
        spread = jnp.where(member[None], value[:, None, :], 0.0)
        return halves(spread.reshape(rank * SEQ_DEV, tokens))

    high_ref[...], low_ref[...] = masked(both[:rank])
    high, low = masked(hid_ref[...])
    right_high, right_low = halves(both[rank:])
    product = mm_nt(high, jnp.concatenate([right_high, right_low], axis=0))
    product = product[:, :rank] + product[:, rank:] + mm_nt(low, right_high)
    product = product.reshape(rank // 2, 2, SEQ_DEV, rank)
    down_ref[...] = jnp.concatenate([product[:, 0], product[:, 1]], axis=2)


def halve_kernel(first, block_ref, half_ref):
    half_ref[...] = block_ref[pl.ds(first, half_ref.shape[0]), : half_ref.shape[1]]


def halve(block, first, tokens):
    shape = (NX // 2, tokens, block.shape[2])
    return call(
        lambda *refs: halve_kernel(first, *refs), jax.ShapeDtypeStruct(shape, block.dtype), [VMEM], (block,), 1, vmem=4
    )


def sort_kernel(w_ref, *out_refs):
    width = w_ref.shape[1] // (NX * NZ)
    z_pos = lax.rem(lax.axis_index("mp"), NZ)
    for steps, out_ref in zip(RING, out_refs):
        for k, step in enumerate(steps):
            place = lax.rem(z_pos + (NZ - step), NZ)
            for x in range(NX):
                column = pl.multiple_of((x * NZ + place) * width, width)
                out_ref[:, pl.ds((k * NX + x) * width, width)] = w_ref[:, pl.ds(column, width)]


def rows(block_ref, tokens):
    return jnp.concatenate([block_ref[i, :tokens] for i in range(block_ref.shape[0])], axis=1)


def first_kernel(w_ref, block_ref, total_ref):
    total_ref[...] = mm_nt(rows(block_ref, total_ref.shape[0]), w_ref[...])


def pair_kernel(w_ref, up_ref, down_ref, total_in, both_in, total_ref, both_ref):
    tokens, deep = total_in.shape[0], both_in.shape[0]
    left = jnp.concatenate([rows(up_ref, tokens), rows(down_ref, tokens)], axis=1)
    total_ref[...] = total_in[...] + mm_nt(left, w_ref[...])
    both = both_in[...]
    for block in (up_ref, down_ref):
        parts = jnp.concatenate([block[x, tokens:] for x in range(NX)], axis=0).astype(F32)
        both += parts[:deep] + parts[deep:]
    both_ref[...] = both


def add_pair(w_part, up, down, total, both):
    return call(
        pair_kernel,
        (jax.ShapeDtypeStruct(total.shape, F32), jax.ShapeDtypeStruct(both.shape, F32)),
        [VMEM] * 5,
        (w_part, up, down, total, both),
        4 * w_part.shape[0] * up.size,
        {3: 0, 4: 1},
    )


def last_kernel(
    w_ref, up_piece, down_piece, total_ref, activated_ref, slope_ref, gate_proj, up_proj, high_ref, low_ref, down_ref,
    sent_ref,
):
    tokens = total_ref.shape[0]
    left = jnp.concatenate([rows(up_piece, tokens), rows(down_piece, tokens)], axis=1)
    hidden_grad = total_ref[...] + mm_nt(left, w_ref[...])
    gate_grad = (hidden_grad * slope_ref[...]).astype(BF16)
    upward_grad = (hidden_grad * activated_ref[...]).astype(BF16)
    factors = jnp.concatenate([mm_nt(gate_grad, gate_proj[...]), mm_nt(upward_grad, up_proj[...])], axis=1)
    high, low = halves(factors)
    product = mm(high_ref[...], jnp.concatenate([high, low], axis=1))
    wide = factors.shape[1]
    product = product[:, :wide] + product[:, wide:] + mm(low_ref[...], high)
    devices = sent_ref.shape[0]
    product = product.reshape(devices, 2 * SEQ_DEV, wide)
    sent_ref[...] = jnp.concatenate([product, down_ref[...]], axis=1).astype(BF16)


def per_device(
    layer_input,
    gate_pre,
    up_pre,
    out_grad,
    w_down,
    proj_input,
    proj_hidden,
    proj_gate,
    proj_upward,
    proj_output,
    seq_ids,
):
    tokens, width = out_grad.shape
    hidden = w_down.shape[0]
    rank = proj_input.shape[1]
    mp_size = lax.axis_size("mp")
    dp_size = lax.axis_size("dp")

    def shape(dims, dtype=F32):
        return jax.ShapeDtypeStruct(dims, dtype)

    deep, share = 2 * rank, tokens // NX
    sent = call(
        start_kernel,
        shape((NX, tokens + 2 * deep, width), BF16),
        [HBM] * 4,
        (layer_input, out_grad, proj_input.T, proj_output),
        4 * tokens * width * rank,
        scratch=[
            pltpu.VMEM((tokens, width), BF16),
            pltpu.VMEM((tokens, width), BF16),
            pltpu.VMEM((rank, width), BF16),
            pltpu.VMEM((rank, width), BF16),
            pltpu.SemaphoreType.DMA((4,)),
        ],
        vmem=56,
    )
    got = lax.all_to_all(sent, "mp", 0, 0, axis_index_groups=X_GROUPS)
    activated, slope, hid_part = call(
        hidden_kernel,
        (shape((tokens, hidden)), shape((tokens, hidden)), shape((rank, tokens))),
        [VMEM] * 3,
        (gate_pre.T, up_pre.T, proj_hidden.T),
        2 * tokens * hidden * rank,
    )
    w_parts = call(
        sort_kernel, [shape((hidden, len(steps) * NX * width), BF16) for steps in RING], [VMEM], (w_down,), w_down.size
    )
    got = tie(got, hid_part, *w_parts)
    across_x, both, parts = call(
        split_kernel,
        (
            shape((NX, tokens + 2 * deep // NX, width), BF16),
            shape((deep, share)),
            shape((2 * deep, share), BF16),
        ),
        [VMEM],
        (got,),
        got.size,
    )
    far_parts = lax.ppermute(parts, "mp", z_shift(NZ // 2))

    up = down = across_x
    next_up, next_down = lax.ppermute(up, "mp", z_shift(1)), lax.ppermute(down, "mp", z_shift(-1))
    total = call(
        first_kernel, shape((tokens, hidden)), [VMEM] * 2, (w_parts[0], across_x), 2 * hidden * across_x.size
    )
    next_up = tie(next_up, total)
    for step in (1, 2):
        up, down = next_up, next_down
        next_up, next_down = lax.ppermute(up, "mp", z_shift(1)), lax.ppermute(down, "mp", z_shift(-1))
        total, both = add_pair(w_parts[step], up, down, total, both)
        next_up = tie(next_up, total)

    up, down = next_up, next_down
    far_up = lax.ppermute(halve(up, 0, tokens), "mp", z_shift(1))
    far_down = lax.ppermute(halve(down, NX // 2, tokens), "mp", z_shift(-1))
    total, both = add_pair(w_parts[3], up, down, total, both)
    both = call(spread_kernel, shape((NX, deep, share)), [VMEM] * 2, (both, far_parts), 1)
    shared = lax.all_to_all(both, "mp", 0, 0, axis_index_groups=X_GROUPS)
    high, low, down_raw = call(
        factor_kernel,
        (
            shape((rank * SEQ_DEV, tokens), BF16),
            shape((rank * SEQ_DEV, tokens), BF16),
            shape((mp_size, SEQ_DEV, 2 * rank)),
        ),
        [VMEM] * 3,
        (shared, hid_part, seq_ids),
        6 * SEQ_DEV * tokens * rank * rank,
    )
    sent = call(
        last_kernel,
        shape((mp_size, 3 * SEQ_DEV, 2 * rank), BF16),
        [VMEM] * 11,
        (
            w_parts[4], far_up, far_down, total, activated, slope, proj_gate.T, proj_upward.T, high, low, down_raw,
        ),
        2 * tokens * hidden * (NX * width + 2 * rank),
        vmem=16,
    )
    got = jnp.sum(lax.all_to_all(sent, "mp", 0, 0).astype(F32), axis=0)
    paired, down_raw = got[: 2 * SEQ_DEV], got[2 * SEQ_DEV :]
    paired = paired.reshape(2, SEQ_DEV, 2, rank).transpose(1, 2, 0, 3).reshape(SEQ_DEV, 2, 2 * rank)
    raw = jnp.concatenate([paired, down_raw[:, None]], axis=1)

    squares = jnp.sum(raw * raw, axis=(0, 2))
    squares = jnp.pad(squares, (0, 125)).reshape(1, 1, 128)
    for axis, size in (("mp", mp_size), ("dp", dp_size)):
        squares = jnp.sum(
            lax.all_to_all(jnp.broadcast_to(squares, (size, 1, 128)), axis, 0, 0), axis=0, keepdims=True
        )
    entries = SEQ_DEV * dp_size * rank * rank
    scale = lax.rsqrt(squares[0, 0, :3] / entries + 1e-06)
    return raw * scale[None, :, None]


def solution(mesh):
    in_specs = (
        P("dp", "mp"),
        P("dp", "mp"),
        P("dp", "mp"),
        P("dp", "mp"),
        P("mp", None),
        P("mp", None),
        P("mp", None),
        P("mp", None),
        P("mp", None),
        P(None, "mp"),
        P("dp", None),
    )
    out_specs = P("dp", None, "mp")
    return jax.shard_map(
        per_device, mesh=mesh, in_specs=in_specs, out_specs=out_specs, check_vma=False
    )
```

```python
import jax
import jax.numpy as jnp
from jax import lax
from jax.experimental import pallas as pl
from jax.experimental.pallas import tpu as pltpu
from jax.sharding import PartitionSpec as P

SEQ_DEV = 8
NX = 4
NZ = 8
X_GROUPS = [[x * NZ + z for x in range(NX)] for z in range(NZ)]
F32, BF16 = jnp.float32, jnp.bfloat16
VMEM = pl.BlockSpec(memory_space=pltpu.VMEM)
HBM = pl.BlockSpec(memory_space=pltpu.HBM)
MIB = 1024 * 1024


def z_shift(step):
    return [(x * NZ + z, x * NZ + (z + step) % NZ) for x in range(NX) for z in range(NZ)]


PARTNER = [(x * NZ + z, (x ^ 1) * NZ + z) for x in range(NX) for z in range(NZ)]
OPPOSITE = [(x * NZ + z, (x ^ 2) * NZ + z) for x in range(NX) for z in range(NZ)]


def place():
    position = lax.axis_index("mp")
    x_pos = lax.div(position, NZ)
    return x_pos, lax.rem(position, NZ), lax.rem(x_pos, 2), lax.rem(lax.axis_index("dp"), 2)


def span(index, size):
    return pl.ds(pl.multiple_of(index * size, size), size)


def quarters(ref, parity):
    share = ref.shape[1] // NX
    return jnp.concatenate([ref[:, span(parity, share)], ref[:, span(parity + 2, share)]], axis=1)


def mm(left, right):
    return jnp.dot(left, right, preferred_element_type=F32)


def mm_nt(left, right):
    return lax.dot_general(left, right, (((1,), (1,)), ((), ())), preferred_element_type=F32)


def halves(value):
    high = value.astype(BF16)
    return high, (value - high.astype(F32)).astype(BF16)


def tie(value, *others):
    return lax.optimization_barrier((value, *others))[0]


def call(kernel, out_shape, specs, operands, flops, aliases=None, scratch=(), vmem=8, out_specs=None):
    size = sum(x.size * x.dtype.itemsize for x in operands)
    return pl.pallas_call(
        kernel,
        out_shape=out_shape,
        in_specs=specs,
        out_specs=out_specs or jax.tree.map(lambda _: VMEM, out_shape),
        scratch_shapes=scratch,
        input_output_aliases=aliases or {},
        cost_estimate=pl.CostEstimate(flops=flops, bytes_accessed=size, transcendentals=0),
        compiler_params=pltpu.CompilerParams(vmem_limit_bytes=vmem * MIB),
    )(*operands)


def fetch(pairs, sems):
    copies = [pltpu.make_async_copy(source, target, sems.at[k]) for k, (source, target) in enumerate(pairs)]
    for copy in copies:
        copy.start()
    return copies


def wait(copies):
    for copy in copies:
        copy.wait()


def start_kernel(
    input_hbm, grad_hbm, gate_hbm, up_hbm, proj_in_hbm, proj_out_hbm, proj_hid_hbm, sent_ref,
    input_ref, grad_ref, gate_ref, up_ref, proj_in_ref, proj_out_ref, proj_hid_ref, sems,
):
    copies = fetch(
        [
            (grad_hbm, grad_ref),
            (proj_out_hbm, proj_out_ref),
            (input_hbm, input_ref),
            (proj_in_hbm, proj_in_ref),
            (gate_hbm, gate_ref),
            (up_hbm, up_ref),
            (proj_hid_hbm, proj_hid_ref),
        ],
        sems,
    )
    wait(copies[:4])
    grad = grad_ref[...]
    factors = [mm_nt(proj_in_ref[...], input_ref[...]), mm_nt(proj_out_ref[...], grad)]
    wait(copies[4:])
    gate = gate_ref[...].astype(F32)
    hidden = gate * jax.nn.sigmoid(gate) * up_ref[...].astype(F32)
    factors.append(mm(proj_hid_ref[...], hidden.astype(BF16)))
    factors = jnp.concatenate(factors, axis=0)
    share = factors.shape[1] // NX
    for x in range(NX):
        own = [grad[k * share : (k + 1) * share] for k in (x % 2, x % 2 + 2)]
        sent_ref[x] = jnp.concatenate([*own, *halves(factors[:, x * share : (x + 1) * share])], axis=0)


def lend_kernel(w_hbm, gate_ref, up_ref, gate_proj, up_proj, lent_ref, sems):
    _, _, own, core = place()
    rows, features = lent_ref.shape[0], w_hbm.shape[1]
    half = gate_ref.shape[1] // 2
    copies = fetch([(w_hbm.at[span(core, rows)], lent_ref.at[:, :features])], sems)
    proj = jnp.concatenate([gate_proj[...], up_proj[...]], axis=0).astype(F32).T.astype(BF16)
    gate, up = quarters(gate_ref, 1 - own), quarters(up_ref, 1 - own)
    for k in range(2):
        part, first = slice(k * rows, (k + 1) * rows), features + k * (lent_ref.shape[1] - features) // 2
        lent_ref[:, first : first + half] = gate[part]
        lent_ref[:, first + half : first + 2 * half] = up[part]
        lent_ref[:, first + 2 * half : first + 2 * half + proj.shape[1]] = proj[part]
    wait(copies)


def split_kernel(got_ref, block_ref, both_ref):
    deep = both_ref.shape[0]
    tokens = got_ref.shape[1] - 2 * deep
    both = got_ref[:, tokens : tokens + deep].astype(F32) + got_ref[:, tokens + deep :].astype(F32)
    both = jnp.sum(both, axis=0)
    both_ref[...] = both
    block_ref[:, :tokens] = got_ref[:, :tokens]
    block_ref[:, tokens:] = jnp.concatenate(halves(both), axis=0).reshape(NX, -1, both.shape[1])


def slopes(gate, up):
    sigmoid = jax.nn.sigmoid(gate)
    return gate * sigmoid, up * (sigmoid * (1.0 + gate * (1.0 - sigmoid)))


def hidden_kernel(gate_ref, up_ref, activated_ref, slope_ref):
    _, _, own, _ = place()
    gate, up = quarters(gate_ref, own), quarters(up_ref, own)
    activated_ref[...], slope_ref[...] = slopes(gate.T.astype(F32), up.T.astype(F32))


def lent_kernel(features, lent_ref, activated_ref, slope_ref, proj_ref):
    _, _, _, core = place()
    half, wide = activated_ref.shape[0], (lent_ref.shape[1] - features) // 2
    parts = [lent_ref[:, pl.ds(pl.multiple_of(features + k * wide, 128), wide)] for k in (core, 1 - core)]
    lent = jnp.concatenate(parts, axis=0)
    gate = lent[:, :half].T.astype(F32)
    up = lent[:, half : 2 * half].T.astype(F32)
    activated_ref[...], slope_ref[...] = slopes(gate, up)
    proj_ref[...] = lent[:, 2 * half :]


def masked(value, ids, member=True):
    count, tokens = value.shape
    member = member & (ids == lax.broadcasted_iota(jnp.int32, (SEQ_DEV, tokens), 0))
    spread = jnp.where(member[None], value[:, None, :], 0.0)
    return halves(spread.reshape(count * SEQ_DEV, tokens))


def left_kernel(own_ref, other_ref, ids_ref, high_ref, low_ref):
    x_pos, _, parity, _ = place()
    first = x_pos < 2
    own, other = own_ref[...], other_ref[...]
    left = jnp.concatenate([jnp.where(first, own, other), jnp.where(first, other, own)], axis=1)
    high_ref[...], low_ref[...] = masked(left, quarters(ids_ref, parity))


def put(grad_ref, block_ref, step):
    _, z_pos, _, _ = place()
    tokens, width = grad_ref.shape[0], block_ref.shape[2]
    came = lax.rem(z_pos + (NZ - step), NZ)
    for x in range(block_ref.shape[0]):
        grad_ref[:, span(x * NZ + came, width)] = block_ref[x, :tokens]


def first_kernel(block_ref, grad_ref):
    put(grad_ref, block_ref, 0)


def add_parts(both, block_ref, tokens):
    deep = both.shape[0]
    parts = jnp.concatenate([block_ref[x, tokens:] for x in range(NX)], axis=0).astype(F32)
    return both + (parts[:deep] + parts[deep:])


def pair_kernel(step, up_ref, down_ref, grad_in, both_in, grad_ref, both_ref):
    tokens = grad_ref.shape[0]
    put(grad_ref, up_ref, step)
    put(grad_ref, down_ref, -step)
    both_ref[...] = add_parts(add_parts(both_in[...], up_ref, tokens), down_ref, tokens)


def far_kernel(block_ref, grad_in, both_ref, ids_ref, grad_ref, in_ref, down_ref):
    tokens, rank = grad_ref.shape[0], in_ref.shape[0]
    x_pos, z_pos, _, _ = place()
    put(grad_ref, block_ref, NZ // 2)
    both = add_parts(both_ref[...], block_ref, tokens)
    share = both.shape[1]
    in_ref[...] = both[:rank]
    own = lax.div(lax.broadcasted_iota(jnp.int32, (SEQ_DEV, share), 1), share // NZ) == z_pos
    high, low = masked(both[2 * rank :], ids_ref[:, span(x_pos, share)], own)
    right_high, right_low = halves(both[rank : 2 * rank])
    product = mm_nt(high, jnp.concatenate([right_high, right_low], axis=0))
    product = product[:, :rank] + product[:, rank:] + mm_nt(low, right_high)
    product = product.reshape(rank // 2, 2, SEQ_DEV, rank)
    down_ref[...] = jnp.concatenate([product[:, 0], product[:, 1]], axis=2)


def add_pair(step, up, down, grad, both):
    return call(
        lambda *refs: pair_kernel(step, *refs),
        (jax.ShapeDtypeStruct(grad.shape, BF16), jax.ShapeDtypeStruct(both.shape, F32)),
        [VMEM] * 4,
        (up, down, grad, both),
        2 * up.size,
        {2: 0, 3: 1},
    )


def own_kernel(grad_ref, w_ref, activated_ref, slope_ref, gate_proj, up_proj, out_ref):
    hidden_grad = mm_nt(grad_ref[...], w_ref[...])
    gate_grad = (hidden_grad * slope_ref[...]).astype(BF16)
    upward_grad = (hidden_grad * activated_ref[...]).astype(BF16)
    out_ref[...] = jnp.concatenate(
        [mm_nt(gate_grad, gate_proj[...]), mm_nt(upward_grad, up_proj[...])], axis=1
    )


def partner_kernel(grad_ref, near_w, far_w, activated_ref, slope_ref, proj_ref, own_ref, out_ref):
    grad = grad_ref[...]
    wide = grad.shape[1]
    hidden_grad = jnp.concatenate([mm_nt(grad, near_w[:, :wide]), mm_nt(grad, far_w[:, :wide])], axis=1)
    gate_grad = (hidden_grad * slope_ref[...]).astype(BF16)
    upward_grad = (hidden_grad * activated_ref[...]).astype(BF16)
    rank = proj_ref.shape[1] // 2
    lent = jnp.concatenate(
        [mm(gate_grad, proj_ref[:, :rank]), mm(upward_grad, proj_ref[:, rank:])], axis=1
    )
    out_ref[...] = own_ref[...] + lent


def last_kernel(total_ref, high_ref, low_ref, down_ref, sent_ref):
    total = total_ref[...]
    high, low = halves(total)
    product = mm(high_ref[...], jnp.concatenate([high, low], axis=1))
    wide = total.shape[1]
    product = product[:, :wide] + product[:, wide:] + mm(low_ref[...], high)
    devices = sent_ref.shape[0]
    sent_ref[:, : 2 * SEQ_DEV] = product.reshape(devices, 2 * SEQ_DEV, wide)
    sent_ref[:, 2 * SEQ_DEV :] = down_ref[...]


def per_device(
    layer_input,
    gate_pre,
    up_pre,
    out_grad,
    w_down,
    proj_input,
    proj_hidden,
    proj_gate,
    proj_upward,
    proj_output,
    seq_ids,
):
    tokens, width = out_grad.shape
    half = tokens // 2
    hidden, features = w_down.shape
    rank = proj_input.shape[1]
    mp_size = lax.axis_size("mp")
    dp_size = lax.axis_size("dp")
    cores = [(k, k ^ 1) for k in range(dp_size)]

    def shape(dims, dtype=F32):
        return jax.ShapeDtypeStruct(dims, dtype)

    gate_turned, up_turned = gate_pre.T, up_pre.T
    deep, share = 3 * rank, tokens // NX
    sent = call(
        start_kernel,
        shape((NX, half + 2 * deep, width), BF16),
        [HBM] * 7,
        (layer_input, out_grad, gate_turned, up_turned, proj_input.T, proj_output, proj_hidden.T),
        4 * tokens * width * rank + 2 * tokens * hidden * rank,
        scratch=[
            pltpu.VMEM((tokens, width), BF16),
            pltpu.VMEM((tokens, width), BF16),
            pltpu.VMEM((hidden, tokens), BF16),
            pltpu.VMEM((hidden, tokens), BF16),
            pltpu.VMEM((rank, width), BF16),
            pltpu.VMEM((rank, width), BF16),
            pltpu.VMEM((rank, hidden), BF16),
            pltpu.SemaphoreType.DMA((7,)),
        ],
        vmem=56,
    )
    lent_w = tie(w_down, sent)
    lent = call(
        lend_kernel,
        shape((hidden // 2, features + 2 * (tokens + 2 * rank)), BF16),
        [HBM] + [VMEM] * 4,
        (lent_w, gate_turned, up_turned, proj_gate.T, proj_upward.T),
        w_down.size,
        scratch=[pltpu.SemaphoreType.DMA((1,))],
    )
    got = lax.all_to_all(sent, "mp", 0, 0, axis_index_groups=X_GROUPS)
    got, lent = lax.optimization_barrier((got, lent))
    near = lax.ppermute(lent, "mp", PARTNER)
    block, both = call(
        split_kernel,
        (
            shape((NX, half + 2 * deep // NX, width), BF16),
            shape((deep, share)),
        ),
        [VMEM],
        (got,),
        got.size,
    )

    up = down = block
    next_up, next_down = lax.ppermute(up, "mp", z_shift(1)), lax.ppermute(down, "mp", z_shift(-1))
    grad = call(first_kernel, shape((half, features), BF16), [VMEM], (block,), block.size)
    next_up = tie(next_up, grad)

    up, down = next_up, next_down
    next_up, next_down = lax.ppermute(up, "mp", z_shift(1)), lax.ppermute(down, "mp", z_shift(-1))
    grad, both = add_pair(1, up, down, grad, both)
    activated, slope = call(
        hidden_kernel,
        (shape((half, hidden)), shape((half, hidden))),
        [VMEM] * 2,
        (gate_turned, up_turned),
        gate_pre.size,
    )
    next_up = tie(next_up, grad, slope)

    up, down = next_up, next_down
    next_up, next_down = lax.ppermute(up, "mp", z_shift(1)), lax.ppermute(down, "mp", z_shift(-1))
    grad, both = add_pair(2, up, down, grad, both)
    next_up = tie(next_up, grad)

    up, down = lax.optimization_barrier((next_up, next_down))
    far = lax.ppermute(up, "mp", z_shift(1))
    grad, both = add_pair(3, up, down, grad, both)
    grad, in_factor, down_raw = call(
        far_kernel,
        (shape(grad.shape, BF16), shape((rank, share)), shape((mp_size, SEQ_DEV, 2 * rank))),
        [VMEM] * 4,
        (far, grad, both, seq_ids),
        far.size,
        {1: 0},
    )
    other_factor = lax.ppermute(in_factor, "mp", OPPOSITE)
    own_factors = call(
        own_kernel,
        shape((half, 2 * rank)),
        [VMEM] * 6,
        (grad, w_down, activated, slope, proj_gate.T, proj_upward.T),
        2 * half * hidden * features,
    )
    near, other_factor, own_factors = lax.optimization_barrier((near, other_factor, own_factors))
    other = lax.ppermute(near, "dp", cores)
    lent_activated, lent_slope, lent_proj = call(
        lambda *refs: lent_kernel(features, *refs),
        (shape((half, hidden)), shape((half, hidden)), shape((hidden, 2 * rank), BF16)),
        [VMEM],
        (near,),
        lent.size,
    )
    high, low = call(
        left_kernel,
        (shape((rank * SEQ_DEV, half), BF16), shape((rank * SEQ_DEV, half), BF16)),
        [VMEM] * 3,
        (in_factor, other_factor, seq_ids),
        SEQ_DEV * half * rank,
    )
    total = call(
        partner_kernel,
        shape(own_factors.shape),
        [VMEM] * 7,
        (grad, near, other, lent_activated, lent_slope, lent_proj, own_factors),
        2 * half * hidden * features,
    )
    sent = call(
        last_kernel,
        shape((mp_size, 3 * SEQ_DEV, 2 * rank)),
        [VMEM] * 4,
        (total, high, low, down_raw),
        6 * high.size * rank,
    )
    got = jnp.sum(lax.all_to_all(sent, "mp", 0, 0), axis=0)
    paired, down_raw = got[: 2 * SEQ_DEV], got[2 * SEQ_DEV :]
    paired = paired.reshape(2, SEQ_DEV, 2, rank).transpose(1, 2, 0, 3).reshape(SEQ_DEV, 2, 2 * rank)
    raw = jnp.concatenate([paired, down_raw[:, None]], axis=1)

    squares = jnp.sum(raw * raw, axis=(0, 2))
    squares = jnp.pad(squares, (0, 125)).reshape(1, 1, 128)
    for axis, size in (("mp", mp_size), ("dp", dp_size)):
        squares = jnp.sum(
            lax.all_to_all(jnp.broadcast_to(squares, (size, 1, 128)), axis, 0, 0), axis=0, keepdims=True
        )
    entries = SEQ_DEV * dp_size * rank * rank
    scale = lax.rsqrt(squares[0, 0, :3] / entries + 1e-06)
    return raw * scale[None, :, None]


def solution(mesh):
    in_specs = (
        P("dp", "mp"),
        P("dp", "mp"),
        P("dp", "mp"),
        P("dp", "mp"),
        P("mp", None),
        P("mp", None),
        P("mp", None),
        P("mp", None),
        P("mp", None),
        P(None, "mp"),
        P("dp", None),
    )
    out_specs = P("dp", None, "mp")
    return jax.shard_map(
        per_device, mesh=mesh, in_specs=in_specs, out_specs=out_specs, check_vma=False
    )
```

```python
import jax
import jax.numpy as jnp
from jax import lax
from jax.experimental import pallas as pl
from jax.experimental.pallas import tpu as pltpu
from jax.sharding import PartitionSpec as P

SEQ_DEV = 8
NX = 4
NZ = 8
X_GROUPS = [[x * NZ + z for x in range(NX)] for z in range(NZ)]
F32, BF16 = jnp.float32, jnp.bfloat16
VMEM = pl.BlockSpec(memory_space=pltpu.VMEM)
HBM = pl.BlockSpec(memory_space=pltpu.HBM)
MIB = 1024 * 1024


def z_shift(step):
    return [(x * NZ + z, x * NZ + (z + step) % NZ) for x in range(NX) for z in range(NZ)]


PARTNER = [(x * NZ + z, (x ^ 1) * NZ + z) for x in range(NX) for z in range(NZ)]
OPPOSITE = [(x * NZ + z, (x ^ 2) * NZ + z) for x in range(NX) for z in range(NZ)]


def place():
    position = lax.axis_index("mp")
    x_pos = lax.div(position, NZ)
    return x_pos, lax.rem(position, NZ), lax.rem(x_pos, 2), lax.rem(lax.axis_index("dp"), 2)


def span(index, size):
    return pl.ds(pl.multiple_of(index * size, size), size)


def quarters(ref, parity):
    share = ref.shape[1] // NX
    return jnp.concatenate([ref[:, span(parity, share)], ref[:, span(parity + 2, share)]], axis=1)


def mm(left, right):
    return jnp.dot(left, right, preferred_element_type=F32)


def mm_nt(left, right):
    return lax.dot_general(left, right, (((1,), (1,)), ((), ())), preferred_element_type=F32)


def halves(value):
    high = value.astype(BF16)
    return high, (value - high.astype(F32)).astype(BF16)


def tie(value, *others):
    return lax.optimization_barrier((value, *others))[0]


def call(kernel, out_shape, specs, operands, flops, aliases=None, scratch=(), vmem=8, out_specs=None):
    size = sum(x.size * x.dtype.itemsize for x in operands)
    return pl.pallas_call(
        kernel,
        out_shape=out_shape,
        in_specs=specs,
        out_specs=out_specs or jax.tree.map(lambda _: VMEM, out_shape),
        scratch_shapes=scratch,
        input_output_aliases=aliases or {},
        cost_estimate=pl.CostEstimate(flops=flops, bytes_accessed=size, transcendentals=0),
        compiler_params=pltpu.CompilerParams(vmem_limit_bytes=vmem * MIB),
    )(*operands)


def fetch(pairs, sems):
    copies = [pltpu.make_async_copy(source, target, sems.at[k]) for k, (source, target) in enumerate(pairs)]
    for copy in copies:
        copy.start()
    return copies


def wait(copies):
    for copy in copies:
        copy.wait()


def start_kernel(
    input_hbm, grad_hbm, gate_hbm, up_hbm, proj_in_hbm, proj_out_hbm, proj_hid_hbm, sent_ref,
    input_ref, grad_ref, gate_ref, up_ref, proj_in_ref, proj_out_ref, proj_hid_ref, sems,
):
    copies = fetch(
        [
            (grad_hbm, grad_ref),
            (proj_out_hbm, proj_out_ref),
            (input_hbm, input_ref),
            (proj_in_hbm, proj_in_ref),
            (gate_hbm, gate_ref),
            (up_hbm, up_ref),
            (proj_hid_hbm, proj_hid_ref),
        ],
        sems,
    )
    wait(copies[:4])
    grad = grad_ref[...]
    factors = [mm_nt(proj_in_ref[...], input_ref[...]), mm_nt(proj_out_ref[...], grad)]
    wait(copies[4:])
    gate = gate_ref[...].astype(F32)
    hidden = gate * jax.nn.sigmoid(gate) * up_ref[...].astype(F32)
    factors.append(mm(proj_hid_ref[...], hidden.astype(BF16)))
    factors = jnp.concatenate(factors, axis=0)
    share = factors.shape[1] // NX
    for x in range(NX):
        own = [grad[k * share : (k + 1) * share] for k in (x % 2, x % 2 + 2)]
        sent_ref[x] = jnp.concatenate([*own, *halves(factors[:, x * share : (x + 1) * share])], axis=0)


def lend_kernel(w_hbm, gate_ref, up_ref, gate_proj, up_proj, lent_ref, sems):
    _, _, own, core = place()
    rows, features = lent_ref.shape[0], w_hbm.shape[1]
    half = gate_ref.shape[1] // 2
    copies = fetch([(w_hbm.at[span(core, rows)], lent_ref.at[:, :features])], sems)
    gate, up = quarters(gate_ref, 1 - own), quarters(up_ref, 1 - own)
    for k in range(2):
        part, first = slice(k * rows, (k + 1) * rows), features + k * 2 * half
        lent_ref[:, first : first + half] = gate[part]
        lent_ref[:, first + half : first + 2 * half] = up[part]
    proj = jnp.concatenate([gate_proj[...], up_proj[...]], axis=0).astype(F32).T.astype(BF16)
    proj = jnp.where(core == 0, proj[:rows].astype(F32), proj[rows:].astype(F32))
    lent_ref[:, features + 4 * half :] = proj.astype(BF16)
    wait(copies)


def split_kernel(got_ref, block_ref, both_ref, hid_ref):
    rank, deep = hid_ref.shape[0], both_ref.shape[0]
    tokens = got_ref.shape[1] - 2 * (deep + rank)
    both = got_ref[:, tokens : tokens + deep + rank].astype(F32) + got_ref[:, tokens + deep + rank :].astype(F32)
    both = jnp.sum(both, axis=0)
    both_ref[...] = both[:deep]
    hid_ref[...] = both[deep:]
    block_ref[:, :tokens] = got_ref[:, :tokens]
    block_ref[:, tokens:] = jnp.concatenate(halves(both[:deep]), axis=0).reshape(NX, -1, both.shape[1])


def slopes(gate, up):
    sigmoid = jax.nn.sigmoid(gate)
    return gate * sigmoid, up * (sigmoid * (1.0 + gate * (1.0 - sigmoid)))


def hidden_kernel(gate_ref, up_ref, activated_ref, slope_ref):
    _, _, own, _ = place()
    gate, up = quarters(gate_ref, own), quarters(up_ref, own)
    activated_ref[...], slope_ref[...] = slopes(gate.T.astype(F32), up.T.astype(F32))


def lent_kernel(features, lent_ref, activated_ref, slope_ref):
    _, _, _, core = place()
    half = activated_ref.shape[0]
    firsts = [pl.multiple_of(features + index * 2 * half, 2 * half) for index in (core, 1 - core)]
    lent = jnp.concatenate([lent_ref[:, pl.ds(first, 2 * half)] for first in firsts], axis=0)
    gate, up = lent[:, :half].T.astype(F32), lent[:, half:].T.astype(F32)
    activated_ref[...], slope_ref[...] = slopes(gate, up)


def masked(value, ids):
    count, tokens = value.shape
    member = ids == lax.broadcasted_iota(jnp.int32, (SEQ_DEV, tokens), 0)
    spread = jnp.where(member[None], value[:, None, :], 0.0)
    return halves(spread.reshape(count * SEQ_DEV, tokens))


def left_kernel(own_ref, other_ref, ids_ref, high_ref, low_ref):
    x_pos, _, parity, _ = place()
    first = x_pos < 2
    own, other = own_ref[...], other_ref[...]
    left = jnp.concatenate([jnp.where(first, own, other), jnp.where(first, other, own)], axis=1)
    high_ref[...], low_ref[...] = masked(left, quarters(ids_ref, parity))


def put(grad_ref, block_ref, step):
    _, z_pos, _, _ = place()
    tokens, width = grad_ref.shape[0], block_ref.shape[2]
    came = lax.rem(z_pos + (NZ - step), NZ)
    for x in range(block_ref.shape[0]):
        grad_ref[:, span(x * NZ + came, width)] = block_ref[x, :tokens]


def first_kernel(block_ref, grad_ref):
    put(grad_ref, block_ref, 0)


def add_parts(both, block_ref, tokens):
    deep = both.shape[0]
    parts = jnp.concatenate([block_ref[x, tokens:] for x in range(NX)], axis=0).astype(F32)
    return both + (parts[:deep] + parts[deep:])


def pair_kernel(step, up_ref, down_ref, grad_in, both_in, grad_ref, both_ref):
    tokens = grad_ref.shape[0]
    put(grad_ref, up_ref, step)
    put(grad_ref, down_ref, -step)
    both_ref[...] = add_parts(add_parts(both_in[...], up_ref, tokens), down_ref, tokens)


def far_kernel(block_ref, grad_in, both_ref, hid_ref, ids_ref, grad_ref, in_ref, down_ref):
    tokens, rank = grad_ref.shape[0], in_ref.shape[0]
    x_pos, _, _, _ = place()
    put(grad_ref, block_ref, NZ // 2)
    both = add_parts(both_ref[...], block_ref, tokens)
    in_ref[...] = both[:rank]
    high, low = masked(hid_ref[...], ids_ref[:, span(x_pos, both.shape[1])])
    right_high, right_low = halves(both[rank:])
    product = mm_nt(high, jnp.concatenate([right_high, right_low], axis=0))
    product = product[:, :rank] + product[:, rank:] + mm_nt(low, right_high)
    product = product.reshape(rank // 2, 2, SEQ_DEV, rank)
    down_ref[...] = jnp.concatenate([product[:, 0], product[:, 1]], axis=2)


def add_pair(step, up, down, grad, both):
    return call(
        lambda *refs: pair_kernel(step, *refs),
        (jax.ShapeDtypeStruct(grad.shape, BF16), jax.ShapeDtypeStruct(both.shape, F32)),
        [VMEM] * 4,
        (up, down, grad, both),
        7000000000,
        {2: 0, 3: 1},
    )


def own_kernel(grad_ref, w_ref, activated_ref, slope_ref, gate_proj, up_proj, out_ref):
    hidden_grad = mm_nt(grad_ref[...], w_ref[...])
    gate_grad = (hidden_grad * slope_ref[...]).astype(BF16)
    upward_grad = (hidden_grad * activated_ref[...]).astype(BF16)
    out_ref[...] = jnp.concatenate(
        [mm_nt(gate_grad, gate_proj[...]), mm_nt(upward_grad, up_proj[...])], axis=1
    )


def partner_kernel(grad_ref, near_ref, other_ref, activated_ref, slope_ref, own_ref, out_ref):
    grad, lent = grad_ref[...], (near_ref, other_ref)
    features, wide = grad.shape[1], own_ref.shape[1]
    hidden_grad = jnp.concatenate([mm_nt(grad, part[:, :features]) for part in lent], axis=1)
    gate_grad = (hidden_grad * slope_ref[...]).astype(BF16)
    upward_grad = (hidden_grad * activated_ref[...]).astype(BF16)
    proj = jnp.concatenate([part[:, part.shape[1] - wide :] for part in lent], axis=0)
    factors = [mm(gate_grad, proj[:, : wide // 2]), mm(upward_grad, proj[:, wide // 2 :])]
    out_ref[...] = own_ref[...] + jnp.concatenate(factors, axis=1)


def last_kernel(total_ref, high_ref, low_ref, down_ref, sent_ref):
    total = total_ref[...]
    high, low = halves(total)
    product = mm(high_ref[...], jnp.concatenate([high, low], axis=1))
    wide = total.shape[1]
    product = product[:, :wide] + product[:, wide:] + mm(low_ref[...], high)
    devices = sent_ref.shape[0]
    sent_ref[:, : 2 * SEQ_DEV] = product.reshape(devices, 2 * SEQ_DEV, wide)
    sent_ref[:, 2 * SEQ_DEV :] = down_ref[...]


def per_device(
    layer_input,
    gate_pre,
    up_pre,
    out_grad,
    w_down,
    proj_input,
    proj_hidden,
    proj_gate,
    proj_upward,
    proj_output,
    seq_ids,
):
    tokens, width = out_grad.shape
    half = tokens // 2
    hidden, features = w_down.shape
    rank = proj_input.shape[1]
    mp_size = lax.axis_size("mp")
    dp_size = lax.axis_size("dp")
    cores = [(k, k ^ 1) for k in range(dp_size)]

    def shape(dims, dtype=F32):
        return jax.ShapeDtypeStruct(dims, dtype)

    gate_turned, up_turned = gate_pre.T, up_pre.T
    deep, share = 2 * rank, tokens // NX
    sent = call(
        start_kernel,
        shape((NX, half + 2 * (deep + rank), width), BF16),
        [HBM] * 7,
        (layer_input, out_grad, gate_turned, up_turned, proj_input.T, proj_output, proj_hidden.T),
        4 * tokens * width * rank + 2 * tokens * hidden * rank,
        scratch=[
            pltpu.VMEM((tokens, width), BF16),
            pltpu.VMEM((tokens, width), BF16),
            pltpu.VMEM((hidden, tokens), BF16),
            pltpu.VMEM((hidden, tokens), BF16),
            pltpu.VMEM((rank, width), BF16),
            pltpu.VMEM((rank, width), BF16),
            pltpu.VMEM((rank, hidden), BF16),
            pltpu.SemaphoreType.DMA((7,)),
        ],
        vmem=56,
    )
    lent_w = tie(w_down, sent)
    lent = call(
        lend_kernel,
        shape((hidden // 2, features + 4 * half + 2 * rank), BF16),
        [HBM] + [VMEM] * 4,
        (lent_w, gate_turned, up_turned, proj_gate.T, proj_upward.T),
        w_down.size,
        scratch=[pltpu.SemaphoreType.DMA((1,))],
    )
    got = lax.all_to_all(sent, "mp", 0, 0, axis_index_groups=X_GROUPS)
    near = lax.ppermute(lent, "mp", PARTNER)
    got = tie(got, lent)
    block, both, hid = call(
        split_kernel,
        (
            shape((NX, half + 2 * deep // NX, width), BF16),
            shape((deep, share)),
            shape((rank, share)),
        ),
        [VMEM],
        (got,),
        got.size,
    )

    up = down = block
    next_up, next_down = lax.ppermute(up, "mp", z_shift(1)), lax.ppermute(down, "mp", z_shift(-1))
    grad = call(first_kernel, shape((half, features), BF16), [VMEM], (block,), block.size)
    next_up = tie(next_up, grad)

    up, down = next_up, next_down
    next_up, next_down = lax.ppermute(up, "mp", z_shift(1)), lax.ppermute(down, "mp", z_shift(-1))
    grad, both = add_pair(1, up, down, grad, both)
    activated, slope = call(
        hidden_kernel,
        (shape((half, hidden)), shape((half, hidden))),
        [VMEM] * 2,
        (gate_turned, up_turned),
        gate_pre.size,
    )
    next_up = tie(next_up, grad, slope)

    up, down = next_up, next_down
    next_up, next_down = lax.ppermute(up, "mp", z_shift(1)), lax.ppermute(down, "mp", z_shift(-1))
    grad, both = add_pair(2, up, down, grad, both)
    next_up = tie(next_up, grad)

    up, down = lax.optimization_barrier((next_up, next_down))
    far = lax.ppermute(up, "mp", z_shift(1))
    grad, both = add_pair(3, up, down, grad, both)
    grad, in_factor, down_raw = call(
        far_kernel,
        (shape(grad.shape, BF16), shape((rank, share)), shape((mp_size, SEQ_DEV, 2 * rank))),
        [VMEM] * 5,
        (far, grad, both, hid, seq_ids),
        far.size,
        {1: 0},
    )
    other_factor = lax.ppermute(in_factor, "mp", OPPOSITE)
    own_factors = call(
        own_kernel,
        shape((half, 2 * rank)),
        [VMEM] * 6,
        (grad, w_down, activated, slope, proj_gate.T, proj_upward.T),
        2 * half * hidden * features,
    )
    near = tie(near, in_factor)
    other = lax.ppermute(near, "dp", cores)
    lent_activated, lent_slope = call(
        lambda *refs: lent_kernel(features, *refs),
        (shape((half, hidden)), shape((half, hidden))),
        [VMEM],
        (near,),
        lent.size,
    )
    high, low = call(
        left_kernel,
        (shape((rank * SEQ_DEV, half), BF16), shape((rank * SEQ_DEV, half), BF16)),
        [VMEM] * 3,
        (in_factor, other_factor, seq_ids),
        SEQ_DEV * half * rank,
    )
    total = call(
        partner_kernel,
        shape(own_factors.shape),
        [VMEM] * 6,
        (grad, near, other, lent_activated, lent_slope, own_factors),
        2 * half * hidden * features,
    )
    sent = call(
        last_kernel,
        shape((mp_size, 3 * SEQ_DEV, 2 * rank)),
        [VMEM] * 4,
        (total, high, low, down_raw),
        6 * high.size * rank,
    )
    got = jnp.sum(lax.all_to_all(sent, "mp", 0, 0), axis=0)
    paired, down_raw = got[: 2 * SEQ_DEV], got[2 * SEQ_DEV :]
    paired = paired.reshape(2, SEQ_DEV, 2, rank).transpose(1, 2, 0, 3).reshape(SEQ_DEV, 2, 2 * rank)
    raw = jnp.concatenate([paired, down_raw[:, None]], axis=1)

    squares = jnp.sum(raw * raw, axis=(0, 2))
    squares = jnp.pad(squares, (0, 125)).reshape(1, 1, 128)
    for axis, size in (("mp", mp_size), ("dp", dp_size)):
        squares = jnp.sum(
            lax.all_to_all(jnp.broadcast_to(squares, (size, 1, 128)), axis, 0, 0), axis=0, keepdims=True
        )
    entries = SEQ_DEV * dp_size * rank * rank
    scale = lax.rsqrt(squares[0, 0, :3] / entries + 1e-06)
    return raw * scale[None, :, None]


def solution(mesh):
    in_specs = (
        P("dp", "mp"),
        P("dp", "mp"),
        P("dp", "mp"),
        P("dp", "mp"),
        P("mp", None),
        P("mp", None),
        P("mp", None),
        P("mp", None),
        P("mp", None),
        P(None, "mp"),
        P("dp", None),
    )
    out_specs = P("dp", None, "mp")
    return jax.shard_map(
        per_device, mesh=mesh, in_specs=in_specs, out_specs=out_specs, check_vma=False
    )
```

```python
import jax
import jax.numpy as jnp
from jax import lax
from jax.experimental import pallas as pl
from jax.experimental.pallas import tpu as pltpu
from jax.sharding import PartitionSpec as P

SEQ_DEV = 8
NX = 4
NZ = 8
X_GROUPS = [[x * NZ + z for x in range(NX)] for z in range(NZ)]
F32, BF16 = jnp.float32, jnp.bfloat16
VMEM = pl.BlockSpec(memory_space=pltpu.VMEM)
HBM = pl.BlockSpec(memory_space=pltpu.HBM)
MIB = 1024 * 1024


def z_shift(step):
    return [(x * NZ + z, x * NZ + (z + step) % NZ) for x in range(NX) for z in range(NZ)]


PARTNER = [(x * NZ + z, (x ^ 1) * NZ + z) for x in range(NX) for z in range(NZ)]
OPPOSITE = [(x * NZ + z, (x ^ 2) * NZ + z) for x in range(NX) for z in range(NZ)]


def place():
    position = lax.axis_index("mp")
    x_pos = lax.div(position, NZ)
    return x_pos, lax.rem(position, NZ), lax.rem(x_pos, 2), lax.rem(lax.axis_index("dp"), 2)


def span(index, size):
    return pl.ds(pl.multiple_of(index * size, size), size)


def quarters(ref, parity):
    share = ref.shape[1] // NX
    return jnp.concatenate([ref[:, span(parity, share)], ref[:, span(parity + 2, share)]], axis=1)


def mm(left, right):
    return jnp.dot(left, right, preferred_element_type=F32)


def mm_nt(left, right):
    return lax.dot_general(left, right, (((1,), (1,)), ((), ())), preferred_element_type=F32)


def halves(value):
    high = value.astype(BF16)
    return high, (value - high.astype(F32)).astype(BF16)


def tie(value, *others):
    return lax.optimization_barrier((value, *others))[0]


def call(kernel, out_shape, specs, operands, flops, aliases=None, scratch=(), vmem=8, out_specs=None):
    size = sum(x.size * x.dtype.itemsize for x in operands)
    return pl.pallas_call(
        kernel,
        out_shape=out_shape,
        in_specs=specs,
        out_specs=out_specs or jax.tree.map(lambda _: VMEM, out_shape),
        scratch_shapes=scratch,
        input_output_aliases=aliases or {},
        cost_estimate=pl.CostEstimate(flops=flops, bytes_accessed=size, transcendentals=0),
        compiler_params=pltpu.CompilerParams(vmem_limit_bytes=vmem * MIB),
    )(*operands)


def fetch(pairs, sems):
    copies = [pltpu.make_async_copy(source, target, sems.at[k]) for k, (source, target) in enumerate(pairs)]
    for copy in copies:
        copy.start()
    return copies


def wait(copies):
    for copy in copies:
        copy.wait()


def start_kernel(
    input_hbm, grad_hbm, gate_hbm, up_hbm, proj_in_hbm, proj_out_hbm, proj_hid_hbm, sent_ref,
    input_ref, grad_ref, gate_ref, up_ref, proj_in_ref, proj_out_ref, proj_hid_ref, sems,
):
    copies = fetch(
        [
            (grad_hbm, grad_ref),
            (proj_out_hbm, proj_out_ref),
            (input_hbm, input_ref),
            (proj_in_hbm, proj_in_ref),
            (gate_hbm, gate_ref),
            (up_hbm, up_ref),
            (proj_hid_hbm, proj_hid_ref),
        ],
        sems,
    )
    wait(copies[:4])
    grad = grad_ref[...]
    factors = [mm_nt(proj_in_ref[...], input_ref[...]), mm_nt(proj_out_ref[...], grad)]
    wait(copies[4:])
    gate = gate_ref[...].astype(F32)
    hidden = gate * jax.nn.sigmoid(gate) * up_ref[...].astype(F32)
    factors.append(mm(proj_hid_ref[...], hidden.astype(BF16)))
    factors = jnp.concatenate(factors, axis=0)
    share = factors.shape[1] // NX
    for x in range(NX):
        own = [grad[k * share : (k + 1) * share] for k in (x % 2, x % 2 + 2)]
        sent_ref[x] = jnp.concatenate([*own, *halves(factors[:, x * share : (x + 1) * share])], axis=0)


def lend_kernel(w_hbm, gate_ref, up_ref, gate_proj, up_proj, lent_ref, sems):
    _, _, own, core = place()
    rows, features = lent_ref.shape[0], w_hbm.shape[1]
    half = gate_ref.shape[1] // 2
    copies = fetch([(w_hbm.at[span(core, rows)], lent_ref.at[:, :features])], sems)
    gate, up = quarters(gate_ref, 1 - own), quarters(up_ref, 1 - own)
    for k in range(2):
        part, first = slice(k * rows, (k + 1) * rows), features + k * 2 * half
        lent_ref[:, first : first + half] = gate[part]
        lent_ref[:, first + half : first + 2 * half] = up[part]
    proj = jnp.concatenate([gate_proj[...], up_proj[...]], axis=0).astype(F32).T.astype(BF16)
    proj = jnp.where(core == 0, proj[:rows].astype(F32), proj[rows:].astype(F32))
    lent_ref[:, features + 4 * half :] = proj.astype(BF16)
    wait(copies)


def split_kernel(got_ref, block_ref, both_ref, hid_ref):
    rank, deep = hid_ref.shape[0], both_ref.shape[0]
    tokens = got_ref.shape[1] - 2 * (deep + rank)
    both = got_ref[:, tokens : tokens + deep + rank].astype(F32) + got_ref[:, tokens + deep + rank :].astype(F32)
    both = jnp.sum(both, axis=0)
    both_ref[...] = both[:deep]
    hid_ref[...] = both[deep:]
    block_ref[:, :tokens] = got_ref[:, :tokens]
    block_ref[:, tokens:] = jnp.concatenate(halves(both[:deep]), axis=0).reshape(NX, -1, both.shape[1])


def slopes(gate, up):
    sigmoid = jax.nn.sigmoid(gate)
    return gate * sigmoid, up * (sigmoid * (1.0 + gate * (1.0 - sigmoid)))


def hidden_kernel(gate_ref, up_ref, activated_ref, slope_ref):
    _, _, own, _ = place()
    gate, up = quarters(gate_ref, own), quarters(up_ref, own)
    activated_ref[...], slope_ref[...] = slopes(gate.T.astype(F32), up.T.astype(F32))


def lent_kernel(features, lent_ref, activated_ref, slope_ref):
    _, _, _, core = place()
    half = activated_ref.shape[0]
    firsts = [pl.multiple_of(features + index * 2 * half, 2 * half) for index in (core, 1 - core)]
    lent = jnp.concatenate([lent_ref[:, pl.ds(first, 2 * half)] for first in firsts], axis=0)
    gate, up = lent[:, :half].T.astype(F32), lent[:, half:].T.astype(F32)
    activated_ref[...], slope_ref[...] = slopes(gate, up)


def masked(value, ids):
    count, tokens = value.shape
    member = ids == lax.broadcasted_iota(jnp.int32, (SEQ_DEV, tokens), 0)
    spread = jnp.where(member[None], value[:, None, :], 0.0)
    return halves(spread.reshape(count * SEQ_DEV, tokens))


def left_kernel(own_ref, other_ref, ids_ref, high_ref, low_ref):
    x_pos, _, parity, _ = place()
    first = x_pos < 2
    own, other = own_ref[...], other_ref[...]
    left = jnp.concatenate([jnp.where(first, own, other), jnp.where(first, other, own)], axis=1)
    high_ref[...], low_ref[...] = masked(left, quarters(ids_ref, parity))


def put(grad_ref, block_ref, step):
    _, z_pos, _, _ = place()
    tokens, width = grad_ref.shape[0], block_ref.shape[2]
    came = lax.rem(z_pos + (NZ - step), NZ)
    for x in range(block_ref.shape[0]):
        grad_ref[:, span(x * NZ + came, width)] = block_ref[x, :tokens]


def first_kernel(block_ref, grad_ref):
    put(grad_ref, block_ref, 0)


def add_parts(both, block_ref, tokens):
    deep = both.shape[0]
    parts = jnp.concatenate([block_ref[x, tokens:] for x in range(NX)], axis=0).astype(F32)
    return both + (parts[:deep] + parts[deep:])


def pair_kernel(step, up_ref, down_ref, grad_in, both_in, grad_ref, both_ref):
    tokens = grad_ref.shape[0]
    put(grad_ref, up_ref, step)
    put(grad_ref, down_ref, -step)
    both_ref[...] = add_parts(add_parts(both_in[...], up_ref, tokens), down_ref, tokens)


def far_kernel(block_ref, grad_in, both_ref, hid_ref, ids_ref, grad_ref, in_ref, down_ref):
    tokens, rank = grad_ref.shape[0], in_ref.shape[0]
    x_pos, _, _, _ = place()
    put(grad_ref, block_ref, NZ // 2)
    both = add_parts(both_ref[...], block_ref, tokens)
    in_ref[...] = both[:rank]
    high, low = masked(hid_ref[...], ids_ref[:, span(x_pos, both.shape[1])])
    right_high, right_low = halves(both[rank:])
    product = mm_nt(high, jnp.concatenate([right_high, right_low], axis=0))
    product = product[:, :rank] + product[:, rank:] + mm_nt(low, right_high)
    product = product.reshape(rank // 2, 2, SEQ_DEV, rank)
    down_ref[...] = jnp.concatenate([product[:, 0], product[:, 1]], axis=2)


def add_pair(step, up, down, grad, both):
    return call(
        lambda *refs: pair_kernel(step, *refs),
        (jax.ShapeDtypeStruct(grad.shape, BF16), jax.ShapeDtypeStruct(both.shape, F32)),
        [VMEM] * 4,
        (up, down, grad, both),
        6000000000,
        {2: 0, 3: 1},
    )


def own_kernel(grad_ref, w_ref, activated_ref, slope_ref, gate_proj, up_proj, out_ref):
    hidden_grad = mm_nt(grad_ref[...], w_ref[...])
    gate_grad = (hidden_grad * slope_ref[...]).astype(BF16)
    upward_grad = (hidden_grad * activated_ref[...]).astype(BF16)
    out_ref[...] = jnp.concatenate(
        [mm_nt(gate_grad, gate_proj[...]), mm_nt(upward_grad, up_proj[...])], axis=1
    )


def partner_kernel(grad_ref, near_ref, other_ref, activated_ref, slope_ref, own_ref, out_ref):
    grad, lent = grad_ref[...], (near_ref, other_ref)
    features, wide = grad.shape[1], own_ref.shape[1]
    hidden_grad = jnp.concatenate([mm_nt(grad, part[:, :features]) for part in lent], axis=1)
    gate_grad = (hidden_grad * slope_ref[...]).astype(BF16)
    upward_grad = (hidden_grad * activated_ref[...]).astype(BF16)
    proj = jnp.concatenate([part[:, part.shape[1] - wide :] for part in lent], axis=0)
    factors = [mm(gate_grad, proj[:, : wide // 2]), mm(upward_grad, proj[:, wide // 2 :])]
    out_ref[...] = own_ref[...] + jnp.concatenate(factors, axis=1)


def last_kernel(total_ref, high_ref, low_ref, down_ref, sent_ref):
    total = total_ref[...]
    high, low = halves(total)
    product = mm(high_ref[...], jnp.concatenate([high, low], axis=1))
    wide = total.shape[1]
    product = product[:, :wide] + product[:, wide:] + mm(low_ref[...], high)
    devices = sent_ref.shape[0]
    sent_ref[:, : 2 * SEQ_DEV] = product.reshape(devices, 2 * SEQ_DEV, wide)
    sent_ref[:, 2 * SEQ_DEV :] = down_ref[...]


def per_device(
    layer_input,
    gate_pre,
    up_pre,
    out_grad,
    w_down,
    proj_input,
    proj_hidden,
    proj_gate,
    proj_upward,
    proj_output,
    seq_ids,
):
    tokens, width = out_grad.shape
    half = tokens // 2
    hidden, features = w_down.shape
    rank = proj_input.shape[1]
    mp_size = lax.axis_size("mp")
    dp_size = lax.axis_size("dp")
    cores = [(k, k ^ 1) for k in range(dp_size)]

    def shape(dims, dtype=F32):
        return jax.ShapeDtypeStruct(dims, dtype)

    gate_turned, up_turned = gate_pre.T, up_pre.T
    deep, share = 2 * rank, tokens // NX
    sent = call(
        start_kernel,
        shape((NX, half + 2 * (deep + rank), width), BF16),
        [HBM] * 7,
        (layer_input, out_grad, gate_turned, up_turned, proj_input.T, proj_output, proj_hidden.T),
        4 * tokens * width * rank + 2 * tokens * hidden * rank,
        scratch=[
            pltpu.VMEM((tokens, width), BF16),
            pltpu.VMEM((tokens, width), BF16),
            pltpu.VMEM((hidden, tokens), BF16),
            pltpu.VMEM((hidden, tokens), BF16),
            pltpu.VMEM((rank, width), BF16),
            pltpu.VMEM((rank, width), BF16),
            pltpu.VMEM((rank, hidden), BF16),
            pltpu.SemaphoreType.DMA((7,)),
        ],
        vmem=56,
    )
    lent_w = tie(w_down, sent)
    lent = call(
        lend_kernel,
        shape((hidden // 2, features + 4 * half + 2 * rank), BF16),
        [HBM] + [VMEM] * 4,
        (lent_w, gate_turned, up_turned, proj_gate.T, proj_upward.T),
        w_down.size,
        scratch=[pltpu.SemaphoreType.DMA((1,))],
    )
    got = lax.all_to_all(sent, "mp", 0, 0, axis_index_groups=X_GROUPS)
    near = lax.ppermute(lent, "mp", PARTNER)
    got = tie(got, lent)
    block, both, hid = call(
        split_kernel,
        (
            shape((NX, half + 2 * deep // NX, width), BF16),
            shape((deep, share)),
            shape((rank, share)),
        ),
        [VMEM],
        (got,),
        got.size,
    )

    up = down = block
    next_up, next_down = lax.ppermute(up, "mp", z_shift(1)), lax.ppermute(down, "mp", z_shift(-1))
    grad = call(first_kernel, shape((half, features), BF16), [VMEM], (block,), block.size)
    next_up = tie(next_up, grad)

    up, down = next_up, next_down
    next_up, next_down = lax.ppermute(up, "mp", z_shift(1)), lax.ppermute(down, "mp", z_shift(-1))
    grad, both = add_pair(1, up, down, grad, both)
    activated, slope = call(
        hidden_kernel,
        (shape((half, hidden)), shape((half, hidden))),
        [VMEM] * 2,
        (gate_turned, up_turned),
        gate_pre.size,
    )
    next_up = tie(next_up, grad, slope)

    up, down = next_up, next_down
    next_up, next_down = lax.ppermute(up, "mp", z_shift(1)), lax.ppermute(down, "mp", z_shift(-1))
    grad, both = add_pair(2, up, down, grad, both)
    next_up = tie(next_up, grad)

    up, down = next_up, next_down
    far = lax.ppermute(up, "mp", z_shift(1))
    grad, both = add_pair(3, up, down, grad, both)
    grad, in_factor, down_raw = call(
        far_kernel,
        (shape(grad.shape, BF16), shape((rank, share)), shape((mp_size, SEQ_DEV, 2 * rank))),
        [VMEM] * 5,
        (far, grad, both, hid, seq_ids),
        far.size,
        {1: 0},
    )
    other_factor = lax.ppermute(in_factor, "mp", OPPOSITE)
    own_factors = call(
        own_kernel,
        shape((half, 2 * rank)),
        [VMEM] * 6,
        (grad, w_down, activated, slope, proj_gate.T, proj_upward.T),
        2 * half * hidden * features,
    )
    near, other_factor, own_factors = lax.optimization_barrier((near, other_factor, own_factors))
    other = lax.ppermute(near, "dp", cores)
    lent_activated, lent_slope = call(
        lambda *refs: lent_kernel(features, *refs),
        (shape((half, hidden)), shape((half, hidden))),
        [VMEM],
        (near,),
        lent.size,
    )
    high, low = call(
        left_kernel,
        (shape((rank * SEQ_DEV, half), BF16), shape((rank * SEQ_DEV, half), BF16)),
        [VMEM] * 3,
        (in_factor, other_factor, seq_ids),
        SEQ_DEV * half * rank,
    )
    total = call(
        partner_kernel,
        shape(own_factors.shape),
        [VMEM] * 6,
        (grad, near, other, lent_activated, lent_slope, own_factors),
        2 * half * hidden * features,
    )
    sent = call(
        last_kernel,
        shape((mp_size, 3 * SEQ_DEV, 2 * rank)),
        [VMEM] * 4,
        (total, high, low, down_raw),
        6 * high.size * rank,
    )
    got = jnp.sum(lax.all_to_all(sent, "mp", 0, 0), axis=0)
    paired, down_raw = got[: 2 * SEQ_DEV], got[2 * SEQ_DEV :]
    paired = paired.reshape(2, SEQ_DEV, 2, rank).transpose(1, 2, 0, 3).reshape(SEQ_DEV, 2, 2 * rank)
    raw = jnp.concatenate([paired, down_raw[:, None]], axis=1)

    squares = jnp.sum(raw * raw, axis=(0, 2))
    squares = jnp.pad(squares, (0, 125)).reshape(1, 1, 128)
    for axis, size in (("mp", mp_size), ("dp", dp_size)):
        squares = jnp.sum(
            lax.all_to_all(jnp.broadcast_to(squares, (size, 1, 128)), axis, 0, 0), axis=0, keepdims=True
        )
    entries = SEQ_DEV * dp_size * rank * rank
    scale = lax.rsqrt(squares[0, 0, :3] / entries + 1e-06)
    return raw * scale[None, :, None]


def solution(mesh):
    in_specs = (
        P("dp", "mp"),
        P("dp", "mp"),
        P("dp", "mp"),
        P("dp", "mp"),
        P("mp", None),
        P("mp", None),
        P("mp", None),
        P("mp", None),
        P("mp", None),
        P(None, "mp"),
        P("dp", None),
    )
    out_specs = P("dp", None, "mp")
    return jax.shard_map(
        per_device, mesh=mesh, in_specs=in_specs, out_specs=out_specs, check_vma=False
    )
```

```python
import jax
import jax.numpy as jnp
from jax import lax
from jax.experimental import pallas as pl
from jax.experimental.pallas import tpu as pltpu
from jax.sharding import PartitionSpec as P

SEQ_DEV = 8
NX = 4
NZ = 8
X_GROUPS = [[x * NZ + z for x in range(NX)] for z in range(NZ)]
F32, BF16 = jnp.float32, jnp.bfloat16
VMEM = pl.BlockSpec(memory_space=pltpu.VMEM)
HBM = pl.BlockSpec(memory_space=pltpu.HBM)
MIB = 1024 * 1024


def z_shift(step):
    return [(x * NZ + z, x * NZ + (z + step) % NZ) for x in range(NX) for z in range(NZ)]


PARTNER = [(x * NZ + z, (x ^ 1) * NZ + z) for x in range(NX) for z in range(NZ)]
OPPOSITE = [(x * NZ + z, (x ^ 2) * NZ + z) for x in range(NX) for z in range(NZ)]


def place():
    position = lax.axis_index("mp")
    x_pos = lax.div(position, NZ)
    return x_pos, lax.rem(position, NZ), lax.rem(x_pos, 2), lax.rem(lax.axis_index("dp"), 2)


def span(index, size):
    return pl.ds(pl.multiple_of(index * size, size), size)


def quarters(ref, parity):
    share = ref.shape[1] // NX
    return jnp.concatenate([ref[:, span(parity, share)], ref[:, span(parity + 2, share)]], axis=1)


def mm(left, right):
    return jnp.dot(left, right, preferred_element_type=F32)


def mm_nt(left, right):
    return lax.dot_general(left, right, (((1,), (1,)), ((), ())), preferred_element_type=F32)


def halves(value):
    high = value.astype(BF16)
    return high, (value - high.astype(F32)).astype(BF16)


def tie(value, *others):
    return lax.optimization_barrier((value, *others))[0]


def call(kernel, out_shape, specs, operands, flops, aliases=None, scratch=(), vmem=8, out_specs=None):
    size = sum(x.size * x.dtype.itemsize for x in operands)
    return pl.pallas_call(
        kernel,
        out_shape=out_shape,
        in_specs=specs,
        out_specs=out_specs or jax.tree.map(lambda _: VMEM, out_shape),
        scratch_shapes=scratch,
        input_output_aliases=aliases or {},
        cost_estimate=pl.CostEstimate(flops=flops, bytes_accessed=size, transcendentals=0),
        compiler_params=pltpu.CompilerParams(vmem_limit_bytes=vmem * MIB),
    )(*operands)


def fetch(pairs, sems):
    copies = [pltpu.make_async_copy(source, target, sems.at[k]) for k, (source, target) in enumerate(pairs)]
    for copy in copies:
        copy.start()
    return copies


def wait(copies):
    for copy in copies:
        copy.wait()


def start_kernel(
    input_hbm, grad_hbm, gate_hbm, up_hbm, proj_in_hbm, proj_out_hbm, proj_hid_hbm, sent_ref,
    input_ref, grad_ref, gate_ref, up_ref, proj_in_ref, proj_out_ref, proj_hid_ref, sems,
):
    copies = fetch(
        [
            (grad_hbm, grad_ref),
            (proj_out_hbm, proj_out_ref),
            (input_hbm, input_ref),
            (proj_in_hbm, proj_in_ref),
            (gate_hbm, gate_ref),
            (up_hbm, up_ref),
            (proj_hid_hbm, proj_hid_ref),
        ],
        sems,
    )
    wait(copies[:4])
    grad = grad_ref[...]
    factors = [mm_nt(proj_in_ref[...], input_ref[...]), mm_nt(proj_out_ref[...], grad)]
    wait(copies[4:])
    gate = gate_ref[...].astype(F32)
    hidden = gate * jax.nn.sigmoid(gate) * up_ref[...].astype(F32)
    factors.append(mm(proj_hid_ref[...], hidden.astype(BF16)))
    factors = jnp.concatenate(factors, axis=0)
    share = factors.shape[1] // NX
    for x in range(NX):
        own = [grad[k * share : (k + 1) * share] for k in (x % 2, x % 2 + 2)]
        sent_ref[x] = jnp.concatenate([*own, *halves(factors[:, x * share : (x + 1) * share])], axis=0)


def lend_kernel(w_ref, gate_ref, up_ref, gate_proj, up_proj, lent_ref):
    _, _, own, core = place()
    rows, features = lent_ref.shape[0], w_ref.shape[1]
    half = gate_ref.shape[1] // 2
    lent_ref[:, :features] = w_ref[span(core, rows)]
    gate, up = quarters(gate_ref, 1 - own), quarters(up_ref, 1 - own)
    for k in range(2):
        part, first = slice(k * rows, (k + 1) * rows), features + k * 2 * half
        lent_ref[:, first : first + half] = gate[part]
        lent_ref[:, first + half : first + 2 * half] = up[part]
    proj = jnp.concatenate([gate_proj[...], up_proj[...]], axis=0).astype(F32).T.astype(BF16)
    proj = jnp.where(core == 0, proj[:rows].astype(F32), proj[rows:].astype(F32))
    lent_ref[:, features + 4 * half :] = proj.astype(BF16)


def split_kernel(got_ref, block_ref, both_ref, hid_ref):
    rank, deep = hid_ref.shape[0], both_ref.shape[0]
    tokens = got_ref.shape[1] - 2 * (deep + rank)
    both = got_ref[:, tokens : tokens + deep + rank].astype(F32) + got_ref[:, tokens + deep + rank :].astype(F32)
    both = jnp.sum(both, axis=0)
    both_ref[...] = both[:deep]
    hid_ref[...] = both[deep:]
    block_ref[:, :tokens] = got_ref[:, :tokens]
    block_ref[:, tokens:] = jnp.concatenate(halves(both[:deep]), axis=0).reshape(NX, -1, both.shape[1])


def slopes(gate, up):
    sigmoid = jax.nn.sigmoid(gate)
    return gate * sigmoid, up * (sigmoid * (1.0 + gate * (1.0 - sigmoid)))


def hidden_kernel(gate_ref, up_ref, activated_ref, slope_ref):
    _, _, own, _ = place()
    gate, up = quarters(gate_ref, own), quarters(up_ref, own)
    activated_ref[...], slope_ref[...] = slopes(gate.T.astype(F32), up.T.astype(F32))


def lent_kernel(features, lent_ref, activated_ref, slope_ref):
    _, _, _, core = place()
    half = activated_ref.shape[0]
    firsts = [pl.multiple_of(features + index * 2 * half, 2 * half) for index in (core, 1 - core)]
    lent = jnp.concatenate([lent_ref[:, pl.ds(first, 2 * half)] for first in firsts], axis=0)
    gate, up = lent[:, :half].T.astype(F32), lent[:, half:].T.astype(F32)
    activated_ref[...], slope_ref[...] = slopes(gate, up)


def masked(value, ids):
    count, tokens = value.shape
    member = ids == lax.broadcasted_iota(jnp.int32, (SEQ_DEV, tokens), 0)
    spread = jnp.where(member[None], value[:, None, :], 0.0)
    return halves(spread.reshape(count * SEQ_DEV, tokens))


def left_kernel(own_ref, other_ref, ids_ref, high_ref, low_ref):
    x_pos, _, parity, _ = place()
    first = x_pos < 2
    own, other = own_ref[...], other_ref[...]
    left = jnp.concatenate([jnp.where(first, own, other), jnp.where(first, other, own)], axis=1)
    high_ref[...], low_ref[...] = masked(left, quarters(ids_ref, parity))


def put(grad_ref, block_ref, step):
    _, z_pos, _, _ = place()
    tokens, width = grad_ref.shape[0], block_ref.shape[2]
    came = lax.rem(z_pos + (NZ - step), NZ)
    for x in range(block_ref.shape[0]):
        grad_ref[:, span(x * NZ + came, width)] = block_ref[x, :tokens]


def first_kernel(block_ref, grad_ref):
    put(grad_ref, block_ref, 0)


def add_parts(both, block_ref, tokens):
    deep = both.shape[0]
    parts = jnp.concatenate([block_ref[x, tokens:] for x in range(NX)], axis=0).astype(F32)
    return both + (parts[:deep] + parts[deep:])


def pair_kernel(step, up_ref, down_ref, grad_in, both_in, grad_ref, both_ref):
    tokens = grad_ref.shape[0]
    put(grad_ref, up_ref, step)
    put(grad_ref, down_ref, -step)
    both_ref[...] = add_parts(add_parts(both_in[...], up_ref, tokens), down_ref, tokens)


def far_kernel(block_ref, grad_in, both_ref, hid_ref, ids_ref, grad_ref, in_ref, down_ref):
    tokens, rank = grad_ref.shape[0], in_ref.shape[0]
    x_pos, _, _, _ = place()
    put(grad_ref, block_ref, NZ // 2)
    both = add_parts(both_ref[...], block_ref, tokens)
    in_ref[...] = both[:rank]
    high, low = masked(hid_ref[...], ids_ref[:, span(x_pos, both.shape[1])])
    right_high, right_low = halves(both[rank:])
    product = mm_nt(high, jnp.concatenate([right_high, right_low], axis=0))
    product = product[:, :rank] + product[:, rank:] + mm_nt(low, right_high)
    product = product.reshape(rank // 2, 2, SEQ_DEV, rank)
    down_ref[...] = jnp.concatenate([product[:, 0], product[:, 1]], axis=2)


def add_pair(step, up, down, grad, both):
    return call(
        lambda *refs: pair_kernel(step, *refs),
        (jax.ShapeDtypeStruct(grad.shape, BF16), jax.ShapeDtypeStruct(both.shape, F32)),
        [VMEM] * 4,
        (up, down, grad, both),
        6000000000,
        {2: 0, 3: 1},
    )


def own_kernel(grad_ref, w_ref, activated_ref, slope_ref, gate_proj, up_proj, out_ref):
    hidden_grad = mm_nt(grad_ref[...], w_ref[...])
    gate_grad = (hidden_grad * slope_ref[...]).astype(BF16)
    upward_grad = (hidden_grad * activated_ref[...]).astype(BF16)
    out_ref[...] = jnp.concatenate(
        [mm_nt(gate_grad, gate_proj[...]), mm_nt(upward_grad, up_proj[...])], axis=1
    )


def partner_kernel(grad_ref, near_ref, other_ref, activated_ref, slope_ref, own_ref, out_ref):
    grad, lent = grad_ref[...], (near_ref, other_ref)
    features, wide = grad.shape[1], own_ref.shape[1]
    hidden_grad = jnp.concatenate([mm_nt(grad, part[:, :features]) for part in lent], axis=1)
    gate_grad = (hidden_grad * slope_ref[...]).astype(BF16)
    upward_grad = (hidden_grad * activated_ref[...]).astype(BF16)
    proj = jnp.concatenate([part[:, part.shape[1] - wide :] for part in lent], axis=0)
    factors = [mm(gate_grad, proj[:, : wide // 2]), mm(upward_grad, proj[:, wide // 2 :])]
    out_ref[...] = own_ref[...] + jnp.concatenate(factors, axis=1)


def last_kernel(total_ref, high_ref, low_ref, down_ref, sent_ref):
    total = total_ref[...]
    high, low = halves(total)
    product = mm(high_ref[...], jnp.concatenate([high, low], axis=1))
    wide = total.shape[1]
    product = product[:, :wide] + product[:, wide:] + mm(low_ref[...], high)
    devices = sent_ref.shape[0]
    product = product.reshape(devices, 2 * SEQ_DEV, wide)
    parts = [product] + [part.astype(F32) for part in halves(down_ref[...])]
    sent_ref[...] = jnp.concatenate(parts, axis=1).astype(BF16)


def per_device(
    layer_input,
    gate_pre,
    up_pre,
    out_grad,
    w_down,
    proj_input,
    proj_hidden,
    proj_gate,
    proj_upward,
    proj_output,
    seq_ids,
):
    tokens, width = out_grad.shape
    half = tokens // 2
    hidden, features = w_down.shape
    rank = proj_input.shape[1]
    mp_size = lax.axis_size("mp")
    dp_size = lax.axis_size("dp")
    cores = [(k, k ^ 1) for k in range(dp_size)]

    def shape(dims, dtype=F32):
        return jax.ShapeDtypeStruct(dims, dtype)

    gate_turned, up_turned = gate_pre.T, up_pre.T
    deep, share = 2 * rank, tokens // NX
    sent = call(
        start_kernel,
        shape((NX, half + 2 * (deep + rank), width), BF16),
        [HBM] * 7,
        (layer_input, out_grad, gate_turned, up_turned, proj_input.T, proj_output, proj_hidden.T),
        4 * tokens * width * rank + 2 * tokens * hidden * rank,
        scratch=[
            pltpu.VMEM((tokens, width), BF16),
            pltpu.VMEM((tokens, width), BF16),
            pltpu.VMEM((hidden, tokens), BF16),
            pltpu.VMEM((hidden, tokens), BF16),
            pltpu.VMEM((rank, width), BF16),
            pltpu.VMEM((rank, width), BF16),
            pltpu.VMEM((rank, hidden), BF16),
            pltpu.SemaphoreType.DMA((7,)),
        ],
        vmem=56,
    )
    lent_w = tie(w_down, sent)
    lent = call(
        lend_kernel,
        shape((hidden // 2, features + 4 * half + 2 * rank), BF16),
        [VMEM] * 5,
        (lent_w, gate_turned, up_turned, proj_gate.T, proj_upward.T),
        w_down.size,
    )
    got = lax.all_to_all(sent, "mp", 0, 0, axis_index_groups=X_GROUPS)
    near = lax.ppermute(lent, "mp", PARTNER)
    got = tie(got, lent)
    block, both, hid = call(
        split_kernel,
        (
            shape((NX, half + 2 * deep // NX, width), BF16),
            shape((deep, share)),
            shape((rank, share)),
        ),
        [VMEM],
        (got,),
        got.size,
    )

    up = down = block
    next_up, next_down = lax.ppermute(up, "mp", z_shift(1)), lax.ppermute(down, "mp", z_shift(-1))
    grad = call(first_kernel, shape((half, features), BF16), [VMEM], (block,), block.size)
    next_up = tie(next_up, grad)

    up, down = next_up, next_down
    next_up, next_down = lax.ppermute(up, "mp", z_shift(1)), lax.ppermute(down, "mp", z_shift(-1))
    grad, both = add_pair(1, up, down, grad, both)
    activated, slope = call(
        hidden_kernel,
        (shape((half, hidden)), shape((half, hidden))),
        [VMEM] * 2,
        (gate_turned, up_turned),
        gate_pre.size,
    )
    next_up = tie(next_up, grad, slope)

    up, down = next_up, next_down
    next_up, next_down = lax.ppermute(up, "mp", z_shift(1)), lax.ppermute(down, "mp", z_shift(-1))
    grad, both = add_pair(2, up, down, grad, both)
    next_up = tie(next_up, grad)

    up, down = next_up, next_down
    far = lax.ppermute(up, "mp", z_shift(1))
    grad, both = add_pair(3, up, down, grad, both)
    grad, in_factor, down_raw = call(
        far_kernel,
        (shape(grad.shape, BF16), shape((rank, share)), shape((mp_size, SEQ_DEV, 2 * rank))),
        [VMEM] * 5,
        (far, grad, both, hid, seq_ids),
        far.size,
        {1: 0},
    )
    other_factor = lax.ppermute(in_factor, "mp", OPPOSITE)
    own_factors = call(
        own_kernel,
        shape((half, 2 * rank)),
        [VMEM] * 6,
        (grad, w_down, activated, slope, proj_gate.T, proj_upward.T),
        2 * half * hidden * features,
    )
    near, other_factor, own_factors = lax.optimization_barrier((near, other_factor, own_factors))
    other = lax.ppermute(near, "dp", cores)
    lent_activated, lent_slope = call(
        lambda *refs: lent_kernel(features, *refs),
        (shape((half, hidden)), shape((half, hidden))),
        [VMEM],
        (near,),
        lent.size,
    )
    high, low = call(
        left_kernel,
        (shape((rank * SEQ_DEV, half), BF16), shape((rank * SEQ_DEV, half), BF16)),
        [VMEM] * 3,
        (in_factor, other_factor, seq_ids),
        SEQ_DEV * half * rank,
    )
    total = call(
        partner_kernel,
        shape(own_factors.shape),
        [VMEM] * 6,
        (grad, near, other, lent_activated, lent_slope, own_factors),
        2 * half * hidden * features,
    )
    sent = call(
        last_kernel,
        shape((mp_size, 4 * SEQ_DEV, 2 * rank), BF16),
        [VMEM] * 4,
        (total, high, low, down_raw),
        6 * high.size * rank,
    )
    got = jnp.sum(lax.all_to_all(sent, "mp", 0, 0).astype(F32), axis=0)
    paired = got[: 2 * SEQ_DEV]
    down_raw = got[2 * SEQ_DEV : 3 * SEQ_DEV] + got[3 * SEQ_DEV :]
    paired = paired.reshape(2, SEQ_DEV, 2, rank).transpose(1, 2, 0, 3).reshape(SEQ_DEV, 2, 2 * rank)
    raw = jnp.concatenate([paired, down_raw[:, None]], axis=1)

    squares = jnp.sum(raw * raw, axis=(0, 2))
    squares = jnp.pad(squares, (0, 125)).reshape(1, 1, 128)
    for axis, size in (("mp", mp_size), ("dp", dp_size)):
        squares = jnp.sum(
            lax.all_to_all(jnp.broadcast_to(squares, (size, 1, 128)), axis, 0, 0), axis=0, keepdims=True
        )
    entries = SEQ_DEV * dp_size * rank * rank
    scale = lax.rsqrt(squares[0, 0, :3] / entries + 1e-06)
    return raw * scale[None, :, None]


def solution(mesh):
    in_specs = (
        P("dp", "mp"),
        P("dp", "mp"),
        P("dp", "mp"),
        P("dp", "mp"),
        P("mp", None),
        P("mp", None),
        P("mp", None),
        P("mp", None),
        P("mp", None),
        P(None, "mp"),
        P("dp", None),
    )
    out_specs = P("dp", None, "mp")
    return jax.shard_map(
        per_device, mesh=mesh, in_specs=in_specs, out_specs=out_specs, check_vma=False
    )
```

```python
import jax
import jax.numpy as jnp
from jax import lax
from jax.experimental import pallas as pl
from jax.experimental.pallas import tpu as pltpu
from jax.sharding import PartitionSpec as P

SEQ_DEV = 8
NX = 4
NZ = 8
X_GROUPS = [[x * NZ + z for x in range(NX)] for z in range(NZ)]
F32, BF16 = jnp.float32, jnp.bfloat16
VMEM = pl.BlockSpec(memory_space=pltpu.VMEM)
HBM = pl.BlockSpec(memory_space=pltpu.HBM)
MIB = 1024 * 1024


def z_shift(step):
    return [(x * NZ + z, x * NZ + (z + step) % NZ) for x in range(NX) for z in range(NZ)]


PARTNER = [(x * NZ + z, (x ^ 1) * NZ + z) for x in range(NX) for z in range(NZ)]
OPPOSITE = [(x * NZ + z, (x ^ 2) * NZ + z) for x in range(NX) for z in range(NZ)]


def place():
    position = lax.axis_index("mp")
    x_pos = lax.div(position, NZ)
    return x_pos, lax.rem(position, NZ), lax.rem(x_pos, 2), lax.rem(lax.axis_index("dp"), 2)


def span(index, size):
    return pl.ds(pl.multiple_of(index * size, size), size)


def quarters(ref, parity):
    share = ref.shape[1] // NX
    return jnp.concatenate([ref[:, span(parity, share)], ref[:, span(parity + 2, share)]], axis=1)


def mm(left, right):
    return jnp.dot(left, right, preferred_element_type=F32)


def mm_nt(left, right):
    return lax.dot_general(left, right, (((1,), (1,)), ((), ())), preferred_element_type=F32)


def halves(value):
    high = value.astype(BF16)
    return high, (value - high.astype(F32)).astype(BF16)


def tie(value, *others):
    return lax.optimization_barrier((value, *others))[0]


def call(kernel, out_shape, specs, operands, flops, aliases=None, scratch=(), vmem=8, out_specs=None):
    size = sum(x.size * x.dtype.itemsize for x in operands)
    return pl.pallas_call(
        kernel,
        out_shape=out_shape,
        in_specs=specs,
        out_specs=out_specs or jax.tree.map(lambda _: VMEM, out_shape),
        scratch_shapes=scratch,
        input_output_aliases=aliases or {},
        cost_estimate=pl.CostEstimate(flops=flops, bytes_accessed=size, transcendentals=0),
        compiler_params=pltpu.CompilerParams(vmem_limit_bytes=vmem * MIB),
    )(*operands)


def fetch(pairs, sems):
    copies = [pltpu.make_async_copy(source, target, sems.at[k]) for k, (source, target) in enumerate(pairs)]
    for copy in copies:
        copy.start()
    return copies


def wait(copies):
    for copy in copies:
        copy.wait()


def start_kernel(
    input_hbm, grad_hbm, gate_hbm, up_hbm, proj_in_hbm, proj_out_hbm, proj_hid_hbm, sent_ref,
    input_ref, grad_ref, gate_ref, up_ref, proj_in_ref, proj_out_ref, proj_hid_ref, sems,
):
    copies = fetch(
        [
            (grad_hbm, grad_ref),
            (proj_out_hbm, proj_out_ref),
            (input_hbm, input_ref),
            (proj_in_hbm, proj_in_ref),
            (gate_hbm, gate_ref),
            (up_hbm, up_ref),
            (proj_hid_hbm, proj_hid_ref),
        ],
        sems,
    )
    wait(copies[:4])
    grad = grad_ref[...]
    factors = [mm_nt(proj_in_ref[...], input_ref[...]), mm_nt(proj_out_ref[...], grad)]
    wait(copies[4:])
    gate = gate_ref[...].astype(F32)
    hidden = gate * jax.nn.sigmoid(gate) * up_ref[...].astype(F32)
    factors.append(mm(proj_hid_ref[...], hidden.astype(BF16)))
    factors = jnp.concatenate(factors, axis=0)
    share = factors.shape[1] // NX
    for x in range(NX):
        own = [grad[k * share : (k + 1) * share] for k in (x % 2, x % 2 + 2)]
        sent_ref[x] = jnp.concatenate([*own, *halves(factors[:, x * share : (x + 1) * share])], axis=0)


def lend_kernel(w_ref, gate_ref, up_ref, gate_proj, up_proj, lent_ref):
    _, _, own, core = place()
    rows, features = lent_ref.shape[0], w_ref.shape[1]
    half = gate_ref.shape[1] // 2
    lent_ref[:, :features] = w_ref[span(core, rows)]
    gate, up = quarters(gate_ref, 1 - own), quarters(up_ref, 1 - own)
    for k in range(2):
        part, first = slice(k * rows, (k + 1) * rows), features + k * 2 * half
        lent_ref[:, first : first + half] = gate[part]
        lent_ref[:, first + half : first + 2 * half] = up[part]
    proj = jnp.concatenate([gate_proj[...], up_proj[...]], axis=0).astype(F32).T.astype(BF16)
    proj = jnp.where(core == 0, proj[:rows].astype(F32), proj[rows:].astype(F32))
    lent_ref[:, features + 4 * half :] = proj.astype(BF16)


def split_kernel(got_ref, block_ref, both_ref, hid_ref):
    rank, deep = hid_ref.shape[0], both_ref.shape[0]
    tokens = got_ref.shape[1] - 2 * (deep + rank)
    both = got_ref[:, tokens : tokens + deep + rank].astype(F32) + got_ref[:, tokens + deep + rank :].astype(F32)
    both = jnp.sum(both, axis=0)
    both_ref[...] = both[:deep]
    hid_ref[...] = both[deep:]
    block_ref[:, :tokens] = got_ref[:, :tokens]
    block_ref[:, tokens:] = jnp.concatenate(halves(both[:deep]), axis=0).reshape(NX, -1, both.shape[1])


def slopes(gate, up):
    sigmoid = jax.nn.sigmoid(gate)
    return gate * sigmoid, up * (sigmoid * (1.0 + gate * (1.0 - sigmoid)))


def hidden_kernel(gate_ref, up_ref, activated_ref, slope_ref):
    _, _, own, _ = place()
    gate, up = quarters(gate_ref, own), quarters(up_ref, own)
    activated_ref[...], slope_ref[...] = slopes(gate.T.astype(F32), up.T.astype(F32))


def lent_kernel(features, lent_ref, activated_ref, slope_ref):
    _, _, _, core = place()
    half = activated_ref.shape[0]
    firsts = [pl.multiple_of(features + index * 2 * half, 2 * half) for index in (core, 1 - core)]
    lent = jnp.concatenate([lent_ref[:, pl.ds(first, 2 * half)] for first in firsts], axis=0)
    gate, up = lent[:, :half].T.astype(F32), lent[:, half:].T.astype(F32)
    activated_ref[...], slope_ref[...] = slopes(gate, up)


def masked(value, ids):
    count, tokens = value.shape
    member = ids == lax.broadcasted_iota(jnp.int32, (SEQ_DEV, tokens), 0)
    spread = jnp.where(member[None], value[:, None, :], 0.0)
    return halves(spread.reshape(count * SEQ_DEV, tokens))


def left_kernel(own_ref, other_ref, ids_ref, high_ref, low_ref):
    x_pos, _, parity, _ = place()
    first = x_pos < 2
    own, other = own_ref[...], other_ref[...]
    left = jnp.concatenate([jnp.where(first, own, other), jnp.where(first, other, own)], axis=1)
    high_ref[...], low_ref[...] = masked(left, quarters(ids_ref, parity))


def put(grad_ref, block_ref, step):
    _, z_pos, _, _ = place()
    tokens, width = grad_ref.shape[0], block_ref.shape[2]
    came = lax.rem(z_pos + (NZ - step), NZ)
    for x in range(block_ref.shape[0]):
        grad_ref[:, span(x * NZ + came, width)] = block_ref[x, :tokens]


def first_kernel(block_ref, grad_ref):
    put(grad_ref, block_ref, 0)


def add_parts(both, block_ref, tokens):
    deep = both.shape[0]
    parts = jnp.concatenate([block_ref[x, tokens:] for x in range(NX)], axis=0).astype(F32)
    return both + (parts[:deep] + parts[deep:])


def pair_kernel(step, up_ref, down_ref, grad_in, both_in, grad_ref, both_ref):
    tokens = grad_ref.shape[0]
    put(grad_ref, up_ref, step)
    put(grad_ref, down_ref, -step)
    both_ref[...] = add_parts(add_parts(both_in[...], up_ref, tokens), down_ref, tokens)


def far_kernel(block_ref, grad_in, both_ref, hid_ref, ids_ref, grad_ref, in_ref, down_ref):
    tokens, rank = grad_ref.shape[0], in_ref.shape[0]
    x_pos, _, _, _ = place()
    put(grad_ref, block_ref, NZ // 2)
    both = add_parts(both_ref[...], block_ref, tokens)
    in_ref[...] = both[:rank]
    high, low = masked(hid_ref[...], ids_ref[:, span(x_pos, both.shape[1])])
    right_high, right_low = halves(both[rank:])
    product = mm_nt(high, jnp.concatenate([right_high, right_low], axis=0))
    product = product[:, :rank] + product[:, rank:] + mm_nt(low, right_high)
    product = product.reshape(rank // 2, 2, SEQ_DEV, rank)
    down_ref[...] = jnp.concatenate([product[:, 0], product[:, 1]], axis=2)


def add_pair(step, up, down, grad, both):
    return call(
        lambda *refs: pair_kernel(step, *refs),
        (jax.ShapeDtypeStruct(grad.shape, BF16), jax.ShapeDtypeStruct(both.shape, F32)),
        [VMEM] * 4,
        (up, down, grad, both),
        6000000000,
        {2: 0, 3: 1},
    )


def own_kernel(grad_ref, w_ref, activated_ref, slope_ref, gate_proj, up_proj, out_ref):
    hidden_grad = mm_nt(grad_ref[...], w_ref[...])
    gate_grad = (hidden_grad * slope_ref[...]).astype(BF16)
    upward_grad = (hidden_grad * activated_ref[...]).astype(BF16)
    out_ref[...] = jnp.concatenate(
        [mm_nt(gate_grad, gate_proj[...]), mm_nt(upward_grad, up_proj[...])], axis=1
    )


def partner_kernel(grad_ref, near_ref, other_ref, activated_ref, slope_ref, own_ref, out_ref):
    grad, lent = grad_ref[...], (near_ref, other_ref)
    features, wide = grad.shape[1], own_ref.shape[1]
    hidden_grad = jnp.concatenate([mm_nt(grad, part[:, :features]) for part in lent], axis=1)
    gate_grad = (hidden_grad * slope_ref[...]).astype(BF16)
    upward_grad = (hidden_grad * activated_ref[...]).astype(BF16)
    proj = jnp.concatenate([part[:, part.shape[1] - wide :] for part in lent], axis=0)
    factors = [mm(gate_grad, proj[:, : wide // 2]), mm(upward_grad, proj[:, wide // 2 :])]
    out_ref[...] = own_ref[...] + jnp.concatenate(factors, axis=1)


def last_kernel(total_ref, high_ref, low_ref, down_ref, sent_ref):
    total = total_ref[...]
    high, low = halves(total)
    product = mm(high_ref[...], jnp.concatenate([high, low], axis=1))
    wide = total.shape[1]
    product = product[:, :wide] + product[:, wide:] + mm(low_ref[...], high)
    devices = sent_ref.shape[0]
    product = product.reshape(devices, 2 * SEQ_DEV, wide)
    parts = [product] + [part.astype(F32) for part in halves(down_ref[...])]
    sent_ref[...] = jnp.concatenate(parts, axis=1).astype(BF16)


def per_device(
    layer_input,
    gate_pre,
    up_pre,
    out_grad,
    w_down,
    proj_input,
    proj_hidden,
    proj_gate,
    proj_upward,
    proj_output,
    seq_ids,
):
    tokens, width = out_grad.shape
    half = tokens // 2
    hidden, features = w_down.shape
    rank = proj_input.shape[1]
    mp_size = lax.axis_size("mp")
    dp_size = lax.axis_size("dp")
    cores = [(k, k ^ 1) for k in range(dp_size)]

    def shape(dims, dtype=F32):
        return jax.ShapeDtypeStruct(dims, dtype)

    gate_turned, up_turned = gate_pre.T, up_pre.T
    deep, share = 2 * rank, tokens // NX
    sent = call(
        start_kernel,
        shape((NX, half + 2 * (deep + rank), width), BF16),
        [HBM] * 7,
        (layer_input, out_grad, gate_turned, up_turned, proj_input.T, proj_output, proj_hidden.T),
        4 * tokens * width * rank + 2 * tokens * hidden * rank,
        scratch=[
            pltpu.VMEM((tokens, width), BF16),
            pltpu.VMEM((tokens, width), BF16),
            pltpu.VMEM((hidden, tokens), BF16),
            pltpu.VMEM((hidden, tokens), BF16),
            pltpu.VMEM((rank, width), BF16),
            pltpu.VMEM((rank, width), BF16),
            pltpu.VMEM((rank, hidden), BF16),
            pltpu.SemaphoreType.DMA((7,)),
        ],
        vmem=56,
    )
    lent_w = tie(w_down, sent)
    lent = call(
        lend_kernel,
        shape((hidden // 2, features + 4 * half + 2 * rank), BF16),
        [VMEM] * 5,
        (lent_w, gate_turned, up_turned, proj_gate.T, proj_upward.T),
        w_down.size,
    )
    got = lax.all_to_all(sent, "mp", 0, 0, axis_index_groups=X_GROUPS)
    near = lax.ppermute(lent, "mp", PARTNER)
    got = tie(got, lent)
    block, both, hid = call(
        split_kernel,
        (
            shape((NX, half + 2 * deep // NX, width), BF16),
            shape((deep, share)),
            shape((rank, share)),
        ),
        [VMEM],
        (got,),
        got.size,
    )

    up = down = block
    next_up, next_down = lax.ppermute(up, "mp", z_shift(1)), lax.ppermute(down, "mp", z_shift(-1))
    grad = call(first_kernel, shape((half, features), BF16), [VMEM], (block,), block.size)
    next_up = tie(next_up, grad)

    up, down = next_up, next_down
    next_up, next_down = lax.ppermute(up, "mp", z_shift(1)), lax.ppermute(down, "mp", z_shift(-1))
    grad, both = add_pair(1, up, down, grad, both)
    activated, slope = call(
        hidden_kernel,
        (shape((half, hidden)), shape((half, hidden))),
        [VMEM] * 2,
        (gate_turned, up_turned),
        gate_pre.size,
    )
    next_up = tie(next_up, grad, slope)

    up, down = next_up, next_down
    next_up, next_down = lax.ppermute(up, "mp", z_shift(1)), lax.ppermute(down, "mp", z_shift(-1))
    grad, both = add_pair(2, up, down, grad, both)
    next_up = tie(next_up, grad)

    up, down = next_up, next_down
    far = lax.ppermute(up, "mp", z_shift(1))
    grad, both = add_pair(3, up, down, grad, both)
    grad, in_factor, down_raw = call(
        far_kernel,
        (shape(grad.shape, BF16), shape((rank, share)), shape((mp_size, SEQ_DEV, 2 * rank))),
        [VMEM] * 5,
        (far, grad, both, hid, seq_ids),
        far.size,
        {1: 0},
    )
    other_factor = lax.ppermute(in_factor, "mp", OPPOSITE)
    own_factors = call(
        own_kernel,
        shape((half, 2 * rank)),
        [VMEM] * 6,
        (grad, w_down, activated, slope, proj_gate.T, proj_upward.T),
        2 * half * hidden * features,
    )
    near = tie(near, in_factor)
    other = lax.ppermute(near, "dp", cores)
    lent_activated, lent_slope = call(
        lambda *refs: lent_kernel(features, *refs),
        (shape((half, hidden)), shape((half, hidden))),
        [VMEM],
        (near,),
        20000000000,
    )
    high, low = call(
        left_kernel,
        (shape((rank * SEQ_DEV, half), BF16), shape((rank * SEQ_DEV, half), BF16)),
        [VMEM] * 3,
        (in_factor, other_factor, seq_ids),
        20000000000,
    )
    total = call(
        partner_kernel,
        shape(own_factors.shape),
        [VMEM] * 6,
        (grad, near, other, lent_activated, lent_slope, own_factors),
        2 * half * hidden * features,
    )
    sent = call(
        last_kernel,
        shape((mp_size, 4 * SEQ_DEV, 2 * rank), BF16),
        [VMEM] * 4,
        (total, high, low, down_raw),
        6 * high.size * rank,
    )
    got = jnp.sum(lax.all_to_all(sent, "mp", 0, 0).astype(F32), axis=0)
    paired = got[: 2 * SEQ_DEV]
    down_raw = got[2 * SEQ_DEV : 3 * SEQ_DEV] + got[3 * SEQ_DEV :]
    paired = paired.reshape(2, SEQ_DEV, 2, rank).transpose(1, 2, 0, 3).reshape(SEQ_DEV, 2, 2 * rank)
    raw = jnp.concatenate([paired, down_raw[:, None]], axis=1)

    squares = jnp.sum(raw * raw, axis=(0, 2))
    squares = jnp.pad(squares, (0, 125)).reshape(1, 1, 128)
    for axis, size in (("mp", mp_size), ("dp", dp_size)):
        squares = jnp.sum(
            lax.all_to_all(jnp.broadcast_to(squares, (size, 1, 128)), axis, 0, 0), axis=0, keepdims=True
        )
    entries = SEQ_DEV * dp_size * rank * rank
    scale = lax.rsqrt(squares[0, 0, :3] / entries + 1e-06)
    return raw * scale[None, :, None]


def solution(mesh):
    in_specs = (
        P("dp", "mp"),
        P("dp", "mp"),
        P("dp", "mp"),
        P("dp", "mp"),
        P("mp", None),
        P("mp", None),
        P("mp", None),
        P("mp", None),
        P("mp", None),
        P(None, "mp"),
        P("dp", None),
    )
    out_specs = P("dp", None, "mp")
    return jax.shard_map(
        per_device, mesh=mesh, in_specs=in_specs, out_specs=out_specs, check_vma=False
    )
```

```python
import jax
import jax.numpy as jnp
from jax import lax
from jax.experimental import pallas as pl
from jax.experimental.pallas import tpu as pltpu
from jax.sharding import PartitionSpec as P

SEQ_DEV = 8
NX = 4
NZ = 8
X_GROUPS = [[x * NZ + z for x in range(NX)] for z in range(NZ)]
F32, BF16 = jnp.float32, jnp.bfloat16
VMEM = pl.BlockSpec(memory_space=pltpu.VMEM)
HBM = pl.BlockSpec(memory_space=pltpu.HBM)
MIB = 1024 * 1024


def z_shift(step):
    return [(x * NZ + z, x * NZ + (z + step) % NZ) for x in range(NX) for z in range(NZ)]


PARTNER = [(x * NZ + z, (x ^ 1) * NZ + z) for x in range(NX) for z in range(NZ)]
OPPOSITE = [(x * NZ + z, (x ^ 2) * NZ + z) for x in range(NX) for z in range(NZ)]


def place():
    position = lax.axis_index("mp")
    x_pos = lax.div(position, NZ)
    return x_pos, lax.rem(position, NZ), lax.rem(x_pos, 2), lax.rem(lax.axis_index("dp"), 2)


def span(index, size):
    return pl.ds(pl.multiple_of(index * size, size), size)


def quarters(ref, parity):
    share = ref.shape[1] // NX
    return jnp.concatenate([ref[:, span(parity, share)], ref[:, span(parity + 2, share)]], axis=1)


def mm(left, right):
    return jnp.dot(left, right, preferred_element_type=F32)


def mm_nt(left, right):
    return lax.dot_general(left, right, (((1,), (1,)), ((), ())), preferred_element_type=F32)


def halves(value):
    high = value.astype(BF16)
    return high, (value - high.astype(F32)).astype(BF16)


def tie(value, *others):
    return lax.optimization_barrier((value, *others))[0]


def call(kernel, out_shape, specs, operands, flops, aliases=None, scratch=(), vmem=8, out_specs=None):
    size = sum(x.size * x.dtype.itemsize for x in operands)
    return pl.pallas_call(
        kernel,
        out_shape=out_shape,
        in_specs=specs,
        out_specs=out_specs or jax.tree.map(lambda _: VMEM, out_shape),
        scratch_shapes=scratch,
        input_output_aliases=aliases or {},
        cost_estimate=pl.CostEstimate(flops=flops, bytes_accessed=size, transcendentals=0),
        compiler_params=pltpu.CompilerParams(vmem_limit_bytes=vmem * MIB),
    )(*operands)


def fetch(pairs, sems):
    copies = [pltpu.make_async_copy(source, target, sems.at[k]) for k, (source, target) in enumerate(pairs)]
    for copy in copies:
        copy.start()
    return copies


def wait(copies):
    for copy in copies:
        copy.wait()


def start_kernel(
    input_hbm, grad_hbm, gate_hbm, up_hbm, proj_in_hbm, proj_out_hbm, proj_hid_hbm, sent_ref,
    input_ref, grad_ref, gate_ref, up_ref, proj_in_ref, proj_out_ref, proj_hid_ref, sems,
):
    copies = fetch(
        [
            (grad_hbm, grad_ref),
            (proj_out_hbm, proj_out_ref),
            (input_hbm, input_ref),
            (proj_in_hbm, proj_in_ref),
            (gate_hbm, gate_ref),
            (up_hbm, up_ref),
            (proj_hid_hbm, proj_hid_ref),
        ],
        sems,
    )
    wait(copies[:4])
    grad = grad_ref[...]
    factors = [mm_nt(proj_in_ref[...], input_ref[...]), mm_nt(proj_out_ref[...], grad)]
    wait(copies[4:])
    gate = gate_ref[...].astype(F32)
    hidden = gate * jax.nn.sigmoid(gate) * up_ref[...].astype(F32)
    factors.append(mm(proj_hid_ref[...], hidden.astype(BF16)))
    factors = jnp.concatenate(factors, axis=0)
    share = factors.shape[1] // NX
    for x in range(NX):
        own = [grad[k * share : (k + 1) * share] for k in (x % 2, x % 2 + 2)]
        sent_ref[x] = jnp.concatenate([*own, *halves(factors[:, x * share : (x + 1) * share])], axis=0)


def lend_kernel(w_ref, gate_ref, up_ref, gate_proj, up_proj, lent_ref):
    _, _, own, core = place()
    rows, features = lent_ref.shape[0], w_ref.shape[1]
    half = gate_ref.shape[1] // 2
    lent_ref[:, :features] = w_ref[span(core, rows)]
    gate, up = quarters(gate_ref, 1 - own), quarters(up_ref, 1 - own)
    for k in range(2):
        part, first = slice(k * rows, (k + 1) * rows), features + k * 2 * half
        lent_ref[:, first : first + half] = gate[part]
        lent_ref[:, first + half : first + 2 * half] = up[part]
    proj = jnp.concatenate([gate_proj[...], up_proj[...]], axis=0).astype(F32).T.astype(BF16)
    proj = jnp.where(core == 0, proj[:rows].astype(F32), proj[rows:].astype(F32))
    lent_ref[:, features + 4 * half :] = proj.astype(BF16)


def split_kernel(got_ref, block_ref, both_ref, hid_ref):
    rank, deep = hid_ref.shape[0], both_ref.shape[0]
    tokens = got_ref.shape[1] - 2 * (deep + rank)
    both = got_ref[:, tokens : tokens + deep + rank].astype(F32) + got_ref[:, tokens + deep + rank :].astype(F32)
    both = jnp.sum(both, axis=0)
    both_ref[...] = both[:deep]
    hid_ref[...] = both[deep:]
    block_ref[:, :tokens] = got_ref[:, :tokens]
    block_ref[:, tokens:] = jnp.concatenate(halves(both[:deep]), axis=0).reshape(NX, -1, both.shape[1])


def slopes(gate, up):
    sigmoid = jax.nn.sigmoid(gate)
    return gate * sigmoid, up * (sigmoid * (1.0 + gate * (1.0 - sigmoid)))


def hidden_kernel(gate_ref, up_ref, activated_ref, slope_ref):
    _, _, own, _ = place()
    gate, up = quarters(gate_ref, own), quarters(up_ref, own)
    activated_ref[...], slope_ref[...] = slopes(gate.T.astype(F32), up.T.astype(F32))


def lent_kernel(features, lent_ref, activated_ref, slope_ref):
    _, _, _, core = place()
    half = activated_ref.shape[0]
    firsts = [pl.multiple_of(features + index * 2 * half, 2 * half) for index in (core, 1 - core)]
    lent = jnp.concatenate([lent_ref[:, pl.ds(first, 2 * half)] for first in firsts], axis=0)
    gate, up = lent[:, :half].T.astype(F32), lent[:, half:].T.astype(F32)
    activated_ref[...], slope_ref[...] = slopes(gate, up)


def masked(value, ids):
    count, tokens = value.shape
    member = ids == lax.broadcasted_iota(jnp.int32, (SEQ_DEV, tokens), 0)
    spread = jnp.where(member[None], value[:, None, :], 0.0)
    return halves(spread.reshape(count * SEQ_DEV, tokens))


def left_kernel(own_ref, other_ref, ids_ref, high_ref, low_ref):
    x_pos, _, parity, _ = place()
    first = x_pos < 2
    own, other = own_ref[...], other_ref[...]
    left = jnp.concatenate([jnp.where(first, own, other), jnp.where(first, other, own)], axis=1)
    high_ref[...], low_ref[...] = masked(left, quarters(ids_ref, parity))


def put(grad_ref, block_ref, step):
    _, z_pos, _, _ = place()
    tokens, width = grad_ref.shape[0], block_ref.shape[2]
    came = lax.rem(z_pos + (NZ - step), NZ)
    for x in range(block_ref.shape[0]):
        grad_ref[:, span(x * NZ + came, width)] = block_ref[x, :tokens]


def first_kernel(block_ref, grad_ref):
    put(grad_ref, block_ref, 0)


def add_parts(both, block_ref, tokens):
    deep = both.shape[0]
    parts = jnp.concatenate([block_ref[x, tokens:] for x in range(NX)], axis=0).astype(F32)
    return both + (parts[:deep] + parts[deep:])


def pair_kernel(step, up_ref, down_ref, grad_in, both_in, grad_ref, both_ref):
    tokens = grad_ref.shape[0]
    put(grad_ref, up_ref, step)
    put(grad_ref, down_ref, -step)
    both_ref[...] = add_parts(add_parts(both_in[...], up_ref, tokens), down_ref, tokens)


def far_kernel(block_ref, grad_in, both_ref, hid_ref, ids_ref, grad_ref, in_ref, down_ref):
    tokens, rank = grad_ref.shape[0], in_ref.shape[0]
    x_pos, _, _, _ = place()
    put(grad_ref, block_ref, NZ // 2)
    both = add_parts(both_ref[...], block_ref, tokens)
    in_ref[...] = both[:rank]
    high, low = masked(hid_ref[...], ids_ref[:, span(x_pos, both.shape[1])])
    right_high, right_low = halves(both[rank:])
    product = mm_nt(high, jnp.concatenate([right_high, right_low], axis=0))
    product = product[:, :rank] + product[:, rank:] + mm_nt(low, right_high)
    product = product.reshape(rank // 2, 2, SEQ_DEV, rank)
    down_ref[...] = jnp.concatenate([product[:, 0], product[:, 1]], axis=2)


def add_pair(step, up, down, grad, both):
    return call(
        lambda *refs: pair_kernel(step, *refs),
        (jax.ShapeDtypeStruct(grad.shape, BF16), jax.ShapeDtypeStruct(both.shape, F32)),
        [VMEM] * 4,
        (up, down, grad, both),
        6000000000,
        {2: 0, 3: 1},
    )


def own_kernel(grad_ref, w_ref, activated_ref, slope_ref, gate_proj, up_proj, out_ref):
    hidden_grad = mm_nt(grad_ref[...], w_ref[...])
    gate_grad = (hidden_grad * slope_ref[...]).astype(BF16)
    upward_grad = (hidden_grad * activated_ref[...]).astype(BF16)
    out_ref[...] = jnp.concatenate(
        [mm_nt(gate_grad, gate_proj[...]), mm_nt(upward_grad, up_proj[...])], axis=1
    )


def partner_kernel(grad_ref, near_ref, other_ref, activated_ref, slope_ref, own_ref, out_ref):
    grad, lent = grad_ref[...], (near_ref, other_ref)
    features, wide = grad.shape[1], own_ref.shape[1]
    hidden_grad = jnp.concatenate([mm_nt(grad, part[:, :features]) for part in lent], axis=1)
    gate_grad = (hidden_grad * slope_ref[...]).astype(BF16)
    upward_grad = (hidden_grad * activated_ref[...]).astype(BF16)
    proj = jnp.concatenate([part[:, part.shape[1] - wide :] for part in lent], axis=0)
    factors = [mm(gate_grad, proj[:, : wide // 2]), mm(upward_grad, proj[:, wide // 2 :])]
    out_ref[...] = own_ref[...] + jnp.concatenate(factors, axis=1)


def last_kernel(total_ref, high_ref, low_ref, down_ref, sent_ref):
    total = total_ref[...]
    high, low = halves(total)
    product = mm(high_ref[...], jnp.concatenate([high, low], axis=1))
    wide = total.shape[1]
    product = product[:, :wide] + product[:, wide:] + mm(low_ref[...], high)
    devices = sent_ref.shape[0]
    product = product.reshape(devices, 2 * SEQ_DEV, wide)
    sent_ref[...] = jnp.concatenate([product, down_ref[...]], axis=1).astype(BF16)


def per_device(
    layer_input,
    gate_pre,
    up_pre,
    out_grad,
    w_down,
    proj_input,
    proj_hidden,
    proj_gate,
    proj_upward,
    proj_output,
    seq_ids,
):
    tokens, width = out_grad.shape
    half = tokens // 2
    hidden, features = w_down.shape
    rank = proj_input.shape[1]
    mp_size = lax.axis_size("mp")
    dp_size = lax.axis_size("dp")
    cores = [(k, k ^ 1) for k in range(dp_size)]

    def shape(dims, dtype=F32):
        return jax.ShapeDtypeStruct(dims, dtype)

    gate_turned, up_turned = gate_pre.T, up_pre.T
    deep, share = 2 * rank, tokens // NX
    sent = call(
        start_kernel,
        shape((NX, half + 2 * (deep + rank), width), BF16),
        [HBM] * 7,
        (layer_input, out_grad, gate_turned, up_turned, proj_input.T, proj_output, proj_hidden.T),
        4 * tokens * width * rank + 2 * tokens * hidden * rank,
        scratch=[
            pltpu.VMEM((tokens, width), BF16),
            pltpu.VMEM((tokens, width), BF16),
            pltpu.VMEM((hidden, tokens), BF16),
            pltpu.VMEM((hidden, tokens), BF16),
            pltpu.VMEM((rank, width), BF16),
            pltpu.VMEM((rank, width), BF16),
            pltpu.VMEM((rank, hidden), BF16),
            pltpu.SemaphoreType.DMA((7,)),
        ],
        vmem=56,
    )
    lent_w = tie(w_down, sent)
    lent = call(
        lend_kernel,
        shape((hidden // 2, features + 4 * half + 2 * rank), BF16),
        [VMEM] * 5,
        (lent_w, gate_turned, up_turned, proj_gate.T, proj_upward.T),
        w_down.size,
    )
    got = lax.all_to_all(sent, "mp", 0, 0, axis_index_groups=X_GROUPS)
    near = lax.ppermute(lent, "mp", PARTNER)
    got = tie(got, lent)
    block, both, hid = call(
        split_kernel,
        (
            shape((NX, half + 2 * deep // NX, width), BF16),
            shape((deep, share)),
            shape((rank, share)),
        ),
        [VMEM],
        (got,),
        got.size,
    )

    up = down = block
    next_up, next_down = lax.ppermute(up, "mp", z_shift(1)), lax.ppermute(down, "mp", z_shift(-1))
    grad = call(first_kernel, shape((half, features), BF16), [VMEM], (block,), block.size)
    next_up = tie(next_up, grad)

    up, down = next_up, next_down
    next_up, next_down = lax.ppermute(up, "mp", z_shift(1)), lax.ppermute(down, "mp", z_shift(-1))
    grad, both = add_pair(1, up, down, grad, both)
    activated, slope = call(
        hidden_kernel,
        (shape((half, hidden)), shape((half, hidden))),
        [VMEM] * 2,
        (gate_turned, up_turned),
        gate_pre.size,
    )
    next_up = tie(next_up, grad, slope)

    up, down = next_up, next_down
    next_up, next_down = lax.ppermute(up, "mp", z_shift(1)), lax.ppermute(down, "mp", z_shift(-1))
    grad, both = add_pair(2, up, down, grad, both)
    next_up = tie(next_up, grad)

    up, down = next_up, next_down
    far = lax.ppermute(up, "mp", z_shift(1))
    grad, both = add_pair(3, up, down, grad, both)
    grad, in_factor, down_raw = call(
        far_kernel,
        (shape(grad.shape, BF16), shape((rank, share)), shape((mp_size, SEQ_DEV, 2 * rank))),
        [VMEM] * 5,
        (far, grad, both, hid, seq_ids),
        far.size,
        {1: 0},
    )
    other_factor = lax.ppermute(in_factor, "mp", OPPOSITE)
    own_factors = call(
        own_kernel,
        shape((half, 2 * rank)),
        [VMEM] * 6,
        (grad, w_down, activated, slope, proj_gate.T, proj_upward.T),
        2 * half * hidden * features,
    )
    near, other_factor, own_factors = lax.optimization_barrier((near, other_factor, own_factors))
    other = lax.ppermute(near, "dp", cores)
    lent_activated, lent_slope = call(
        lambda *refs: lent_kernel(features, *refs),
        (shape((half, hidden)), shape((half, hidden))),
        [VMEM],
        (near,),
        lent.size,
    )
    high, low = call(
        left_kernel,
        (shape((rank * SEQ_DEV, half), BF16), shape((rank * SEQ_DEV, half), BF16)),
        [VMEM] * 3,
        (in_factor, other_factor, seq_ids),
        SEQ_DEV * half * rank,
    )
    total = call(
        partner_kernel,
        shape(own_factors.shape),
        [VMEM] * 6,
        (grad, near, other, lent_activated, lent_slope, own_factors),
        2 * half * hidden * features,
    )
    sent = call(
        last_kernel,
        shape((mp_size, 3 * SEQ_DEV, 2 * rank), BF16),
        [VMEM] * 4,
        (total, high, low, down_raw),
        6 * high.size * rank,
    )
    got = jnp.sum(lax.all_to_all(sent, "mp", 0, 0).astype(F32), axis=0)
    paired, down_raw = got[: 2 * SEQ_DEV], got[2 * SEQ_DEV :]
    paired = paired.reshape(2, SEQ_DEV, 2, rank).transpose(1, 2, 0, 3).reshape(SEQ_DEV, 2, 2 * rank)
    raw = jnp.concatenate([paired, down_raw[:, None]], axis=1)

    squares = jnp.sum(raw * raw, axis=(0, 2))
    squares = jnp.pad(squares, (0, 125)).reshape(1, 1, 128)
    for axis, size in (("mp", mp_size), ("dp", dp_size)):
        squares = jnp.sum(
            lax.all_to_all(jnp.broadcast_to(squares, (size, 1, 128)), axis, 0, 0), axis=0, keepdims=True
        )
    entries = SEQ_DEV * dp_size * rank * rank
    scale = lax.rsqrt(squares[0, 0, :3] / entries + 1e-06)
    return raw * scale[None, :, None]


def solution(mesh):
    in_specs = (
        P("dp", "mp"),
        P("dp", "mp"),
        P("dp", "mp"),
        P("dp", "mp"),
        P("mp", None),
        P("mp", None),
        P("mp", None),
        P("mp", None),
        P("mp", None),
        P(None, "mp"),
        P("dp", None),
    )
    out_specs = P("dp", None, "mp")
    return jax.shard_map(
        per_device, mesh=mesh, in_specs=in_specs, out_specs=out_specs, check_vma=False
    )
```
